768 devices in a mesh: dp: 12 (over z), emb: 64 (over y, x, core).
Axes of the slice: x: 4, y: 8, z: 12, core: 2. Of those that a mesh axis runs over, the one named last changes fastest.
Arguments:
- emb_table: bfloat16 [65536, 192], P('emb'), may hold values from -6 to 6
- requests: int32 [768, 64, 32], P(('dp', 'emb')), may hold values from 0 to 1023
- token_slot: int32 [768, 2048], P(('dp', 'emb')), may hold values from 0 to 2047, each once within a row
- kept_mask: int32 [6144, 256], P(('dp', 'emb')), may hold values 0 or 1
- fm_proj: bfloat16 [256, 96], replicated, may hold values from -0.375 to 0.375
- comp_weight: bfloat16 [256, 256], replicated, may hold values from -0.375 to 0.375
- comp_cotangent: bfloat16 [6144, 49152], P(('dp', 'emb')), may hold values from -6 to 6
Outputs:
- fm_tokens: bfloat16 [6144, 24576], P(('dp', 'emb'))
- compressed: bfloat16 [6144, 49152], P(('dp', 'emb'))
- table_grad: float32 [65536, 192], P('emb')
- weight_grad: float32 [256, 256], replicated
The draws below stay inside these ranges and needn't reach their ends.
Inputs may be any that keep to these rules, and one draw needn't show every extreme that they name: Each device's row of token_slot names every slot once.
All inputs are finite; a program needn't handle non-finite values. No bound on the sum of `kept_mask` on one device may be relied on, other than what follows from the above.
Results may differ from the reference program's by a relative error of at most 0.0038.
Values may be sent and summed in bfloat16 or wider, within the bound.
A program may use at most 32 MiB of HBM per device.

```python
import jax
import jax.numpy as jnp
from jax import lax

D = 192
NTOK = 256
RANK = 96
NCOMP = 256
B_DEV = 8
ROWS_DEV = 1024
TOK_DEV = 2048
CAP = 32
SAMPLES = 6144
TABROWS = 65536
N_EMB = 64
DEVICES = 768


def place_ends(drawn, stream_key, low, top_value):
    shape = drawn.shape
    index_at = [jax.random.randint(jax.random.fold_in(stream_key, axis), (), 0, shape[axis]) for axis in range(len(shape))]
    drawn = drawn.at[tuple(index_at)].set(low)
    longest = shape.index(max(shape))
    index_at[longest] = (index_at[longest] + 1) % shape[longest]
    return drawn.at[tuple(index_at)].set(top_value)


def block_levels(key, dims, cuts, smallest, largest):
    def one(position, shards_of):
        heights = jax.random.uniform(jax.random.fold_in(jax.random.fold_in(key, 6), position), (shards_of,), jnp.float32, smallest / len(cuts), largest / len(cuts))
        return jnp.repeat(jnp.exp(heights), dims[position] // shards_of).reshape((-1,) + (1,) * (len(dims) - position - 1))

    gain = one(*cuts[0])
    for cut in cuts[1:]:
        gain = gain * one(*cut)
    return gain


def scatter_about(stream_key, shape, deviation, most, split=(), kind=jnp.bfloat16):
    drawn = jax.random.normal(stream_key, shape, jnp.float32) * deviation
    if len(split) > 0:
        drawn = block_levels(stream_key, shape, split, -0.22, 0.18) * drawn
    return jnp.clip(drawn, min=-most, max=most).astype(kind)


def setup_inputs(seed: int = 0) -> dict:
    keys = jax.random.split(jax.random.key(seed), 8)
    emb_table = scatter_about(keys[0], (TABROWS, D), 1.0, 6.0, ((0, 64),))
    requests = place_ends(jax.random.randint(keys[1], (DEVICES, N_EMB, CAP), 0, ROWS_DEV), jax.random.fold_in(keys[1], 1), 0, ROWS_DEV - 1).astype(jnp.int32)
    token_slot = jax.vmap(lambda own: jax.random.permutation(own, TOK_DEV))(jax.random.split(keys[2], DEVICES)).reshape((DEVICES, TOK_DEV)).astype(jnp.int32)
    kept_mask = place_ends((jax.random.randint(keys[3], (SAMPLES, NTOK), 0, 4) < 3).astype(jnp.int32), jax.random.fold_in(keys[3], 1), 0, 1)
    fm_proj = scatter_about(keys[4], (NTOK, RANK), NTOK ** -0.5, 0.375)
    comp_weight = scatter_about(keys[5], (NCOMP, NTOK), NTOK ** -0.5, 0.375)
    comp_cotangent = scatter_about(keys[6], (SAMPLES, NCOMP * D), 1.0, 6.0, ((0, 768),))
    return dict(emb_table=emb_table, requests=requests, token_slot=token_slot, kept_mask=kept_mask, fm_proj=fm_proj, comp_weight=comp_weight, comp_cotangent=comp_cotangent)


def reference(emb_table, requests, token_slot, kept_mask, fm_proj, comp_weight, comp_cotangent):
    flat_requests = requests.reshape(DEVICES, N_EMB * CAP)
    owner = token_slot // CAP
    local_rows = jnp.take_along_axis(flat_requests, token_slot, axis=1)
    all_rows = (owner * ROWS_DEV + local_rows).astype(jnp.int32)
    masks = kept_mask.reshape(DEVICES, B_DEV, NTOK)
    cotangents = comp_cotangent.reshape(DEVICES, B_DEV, NCOMP, D)
    proj_f = fm_proj.astype(jnp.float32)
    weight_f = comp_weight.astype(jnp.float32)

    def one_device(carry, inputs):
        table_acc, weight_acc = carry
        rows, mask_block, cot_block = inputs
        gathered = jnp.take(emb_table, rows, axis=0).reshape(B_DEV, NTOK, D)
        embedded = gathered * mask_block[:, :, None].astype(jnp.bfloat16)
        emb_f = embedded.astype(jnp.float32)
        projected = jnp.einsum('bnd,nk->bdk', emb_f, proj_f).astype(jnp.bfloat16)
        fm_raw = jnp.einsum('bnd,bdk->bnk', emb_f, projected.astype(jnp.float32))
        mean = lax.optimization_barrier(jnp.mean(fm_raw, axis=(1, 2), keepdims=True))
        variance = lax.optimization_barrier(jnp.mean((fm_raw - mean) ** 2, axis=(1, 2), keepdims=True))
        normed = ((fm_raw - mean) * lax.rsqrt(variance + 1e-05)).astype(jnp.bfloat16)
        compressed = jnp.einsum('mn,bnd->bmd', weight_f, emb_f).astype(jnp.bfloat16)
        cot_f = cot_block.astype(jnp.float32)
        row_grad = jnp.einsum('mn,bmd->bnd', weight_f, cot_f) * mask_block[:, :, None].astype(jnp.float32)
        table_acc = table_acc.at[rows].add(row_grad.reshape(B_DEV * NTOK, D))
        weight_acc = weight_acc + jnp.einsum('bmd,bnd->mn', cot_f, emb_f)
        return ((table_acc, weight_acc), (normed.reshape(B_DEV, NTOK * RANK), compressed.reshape(B_DEV, NCOMP * D)))
    start = (jnp.zeros((TABROWS, D), jnp.float32), jnp.zeros((NCOMP, NTOK), jnp.float32))
    (table_grad, weight_total), (fm_tokens, compressed) = lax.scan(one_device, start, (all_rows, masks, cotangents))
    weight_grad = weight_total / jnp.float32(SAMPLES)
    return (fm_tokens.reshape(SAMPLES, NTOK * RANK), compressed.reshape(SAMPLES, NCOMP * D), table_grad, weight_grad)
```

```python
import functools

import jax
import jax.numpy as jnp
from jax import lax
from jax.experimental import pallas as pl
from jax.experimental.pallas import tpu as pltpu
from jax.sharding import PartitionSpec as P

MESH = pl.DeviceIdType.MESH
BF = jnp.bfloat16
F32 = jnp.float32
NZ, NY, NX, NC = 12, 8, 4, 2
NP = NY * NX * NC
D, NTOK, RANK, NCOMP, B, ROWS, CAP = 192, 256, 96, 256, 8, 1024, 32
TOK = B * NTOK
PACK = CAP + CAP // 2
SAMPLES = 6144


def dot(a, b):
    return jnp.dot(a, b, preferred_element_type=F32)


def dot_t(a, b):
    return lax.dot_general(a, b, (((1,), (1,)), ((), ())), preferred_element_type=F32)


def onehot(mask):
    return mask.astype(F32).astype(BF)


def alternate(e, n):
    half = (e + 1) // 2
    return lax.rem(jnp.where(lax.rem(e, 2) == 1, half, n - half), n)


def kernel(
    table_t, req_t, slot, mask, proj_t, weight, cot,
    fm_o, comp_o, tg_o, wg_o,
    reqs, reqr, wrow, wcol, slot8, smcol,
    cplane, cb, rg, table, wt,
    bsend, brecv, asend, arecv, ret, arr,
    tgf, zsend, zrecv, zfull,
    weo, bdp, bdc, fplane, mplane,
    wsum, wrecv, wtile, wzrecv, wfin, wfull,
    s_rq, s_b, s_a, s_z, s_w, s_wz, s_wg, s_gs, s_gr,
):
    z = lax.axis_index("dp")
    me = lax.axis_index("emb")
    my = me // (NX * NC)
    mx = lax.rem(me // NC, NX)
    mc = lax.rem(me, NC)

    def peer(j):
        dy = alternate(lax.rem(j, NY), NY)
        dxc = j // NY
        py = lax.rem(my + dy, NY)
        px = lax.rem(mx + dxc // NC, NX)
        pc = lax.rem(mc + dxc, NC)
        return (py * NX + px) * NC + pc

    def zpeer(j):
        return lax.rem(z + alternate(j, NZ), NZ)

    def wait(ref, sem):
        pltpu.make_async_copy(ref, ref, sem).wait()

    def plane_send(src, dst, sems):
        def body(j, carry):
            p = peer(j)
            pltpu.make_async_remote_copy(
                src_ref=src(p), dst_ref=dst, send_sem=sems.at[0], recv_sem=sems.at[1],
                device_id={"emb": p}, device_id_type=MESH,
            ).start()
            return carry
        lax.fori_loop(1, NP, body, 0)

    def z_send(src, dst, sems):
        def body(j, carry):
            p = zpeer(j)
            pltpu.make_async_remote_copy(
                src_ref=src(p), dst_ref=dst, send_sem=sems.at[0], recv_sem=sems.at[1],
                device_id={"dp": p}, device_id_type=MESH,
            ).start()
            return carry
        lax.fori_loop(1, NZ, body, 0)

    barrier = pltpu.get_barrier_semaphore()

    def sig_plane(j, carry):
        pl.semaphore_signal(barrier, inc=1, device_id={"emb": peer(j)}, device_id_type=MESH)
        return carry

    def sig_z(j, carry):
        pl.semaphore_signal(barrier, inc=1, device_id={"dp": zpeer(j)}, device_id_type=MESH)
        return carry

    lax.fori_loop(1, NP, sig_plane, 0)
    lax.fori_loop(1, NZ, sig_z, 0)

    lane = lax.broadcasted_iota(jnp.int32, (1, 128), 1)
    low = lane < 64

    rt = jnp.concatenate([req_t[...], jnp.zeros((128 - CAP, NP), jnp.int32)], 0)
    rt = jnp.concatenate([rt, jnp.zeros((128, 128 - NP), jnp.int32)], 1).T
    rt = rt[0:NP]
    tiled = rt
    for i in range(1, 4):
        tiled = tiled + pltpu.roll(rt, 32 * i, 1)
    tiled = jnp.where(lane // CAP == lax.rem(me, 4), tiled, 0)
    for p in range(NP):
        reqs[p] = tiled[p : p + 1]
    reqr[lax.rem(me, 4) * 16 + me // 4] = reqs[me]

    for b in range(B):
        slot8[b : b + 1, :] = slot[0:1, b * NTOK : (b + 1) * NTOK]
    masked = jnp.where(mask[...] > 0, slot8[...], -1)
    slot8[...] = masked
    smcol[...] = jnp.concatenate([masked, jnp.full((120, NTOK), -1, jnp.int32)], 0).T

    pl.semaphore_wait(barrier, NP - 1 + NZ - 1)
    plane_send(lambda p: reqs.at[p], reqr.at[lax.rem(me, 4) * 16 + me // 4], s_rq)

    def unpack_cot(mp, carry):
        at = pl.multiple_of(mp * 384, 128)
        x = cot[:, pl.ds(at, 384)].astype(F32)
        x0, x1, x2 = x[:, 0:128], x[:, 128:256], x[:, 256:384]
        r1 = pltpu.roll(x1, 64, 1)
        r2 = pltpu.roll(x2, 64, 1)
        ev, od = pl.ds(2 * mp, B, stride=NCOMP), pl.ds(2 * mp + 1, B, stride=NCOMP)
        cplane[0, ev, :] = x0
        cplane[1, ev, :] = jnp.where(low, x1, r1)
        cplane[0, od, :] = jnp.where(low, r1, r2)
        cplane[1, od, :] = jnp.where(low, r2, x2)
        return carry

    lax.fori_loop(0, NCOMP // 2, unpack_cot, 0, unroll=8)
    wt[...] = weight[...].astype(F32).T.astype(BF)

    def make_rg(b, carry):
        rows = pl.ds(pl.multiple_of(b * NCOMP, NCOMP), NCOMP)
        c = jnp.concatenate([cplane[0, rows, :], cplane[1, rows, :]], 1).astype(BF)
        cb[rows, :] = c
        rg[rows, :] = dot(wt[...], c).astype(BF)
        return carry

    lax.fori_loop(0, B, make_rg, 0)

    sub = lax.broadcasted_iota(jnp.int32, (128, 1), 0)

    def packed(val, dst, g):
        for q in range(4):
            v = val[q * CAP : (q + 1) * CAP]
            dst[g * 4 + q, 0:CAP, :] = v[:, 0:128].astype(BF)
            dst[g * 4 + q, CAP:PACK, :] = jnp.where(low, v[0:16, 128:256], v[16:32, 128:256]).astype(BF)

    def order(e, carry):
        g = lax.rem(me // 4 + alternate(e, 16), 16)
        key = sub + g * 128
        pt = jnp.concatenate([onehot(slot8[b : b + 1, :] == key) for b in range(B)], 1)
        packed(dot(pt, rg[...]), bsend, g)
        return carry

    lax.fori_loop(0, 16, order, 0)
    brecv[me] = bsend[me]
    plane_send(lambda p: bsend.at[p], brecv.at[me], s_b)

    for i in range(8):
        blk = table_t[:, i * 128 : (i + 1) * 128].astype(F32)
        blk = jnp.concatenate([blk, blk[128:192]], 0).T
        table[i * 128 : (i + 1) * 128, :] = blk.astype(BF)

    wait(reqr.at[pl.ds(0, NP - 1)], s_rq.at[1])
    for g in range(16):
        wrow[g : g + 1, :] = reqr[g] + reqr[16 + g] + reqr[32 + g] + reqr[48 + g]
    wc = jnp.concatenate([wrow[...], jnp.zeros((112, 128), jnp.int32)], 0).T
    for g in range(16):
        wcol[g] = jnp.broadcast_to(wc[:, g : g + 1], (128, 128))
    rlane = lax.broadcasted_iota(jnp.int32, (1, 128), 1)

    def fetch(e, carry):
        g = lax.rem(me // 4 + alternate(e, 16), 16)
        col = wcol[g]
        o = jnp.concatenate([onehot(col == rlane + 128 * i) for i in range(8)], 1)
        packed(dot(o, table[...]), asend, g)
        return carry

    lax.fori_loop(0, 16, fetch, 0)
    arecv[me] = asend[me]
    plane_send(lambda p: asend.at[p], arecv.at[me], s_a)

    def unpack(src, dst):
        def body(p, carry):
            at = pl.multiple_of(p * CAP, CAP)
            dst[pl.ds(at, CAP), 0:128] = src[p, 0:CAP, :]
            h = src[p, CAP:PACK, :].astype(F32)
            dst[pl.ds(at, 16), 128:256] = jnp.where(low, h, 0.0).astype(BF)
            h = pltpu.roll(h, 64, 1)
            dst[pl.ds(pl.multiple_of(at + 16, 16), 16), 128:256] = jnp.where(low, h, 0.0).astype(BF)
            return carry
        lax.fori_loop(0, NP, body, 0, unroll=4)

    wait(brecv.at[pl.ds(0, NP - 1)], s_b.at[1])
    unpack(brecv, ret)

    def scatter(rb, carry):
        key = sub + rb * 128
        o = jnp.concatenate([onehot(wrow[g : g + 1, :] == key) for g in range(16)], 1)
        t = dot(o, ret[...])
        t = t.T[0:D].reshape(NZ, 16, 128)
        at = pl.ds(pl.multiple_of(rb * 128, 128), 128)
        tgf[:, :, at] = t
        zsend[:, :, at] = t.astype(BF)
        return carry

    lax.fori_loop(0, 8, scatter, 0)
    z_send(lambda p: zsend.at[p], zrecv.at[z], s_z)

    r256 = lax.broadcasted_iota(jnp.int32, (256, 256), 0)
    c256 = lax.broadcasted_iota(jnp.int32, (256, 256), 1)
    q_fm = onehot(c256 == 4 * lax.rem(r256, 64) + r256 // 64)
    q_w = onehot(c256 == 2 * lax.rem(r256, 128) + r256 // 128)
    wp = dot(q_w, weight[...]).astype(BF)
    weo[...] = jnp.concatenate([wp[0:128], wp[128:256]], 1)
    bdp[...] = jnp.zeros_like(bdp)
    bdc[...] = jnp.zeros_like(bdc)
    zlane = lax.broadcasted_iota(jnp.int32, (1, TOK), 1)

    wait(arecv.at[pl.ds(0, NP - 1)], s_a.at[1])
    unpack(arecv, arr)
    wsum[...] = jnp.zeros_like(wsum)
    colid = lax.broadcasted_iota(jnp.int32, (NTOK, 128), 1)

    def forward(b, carry):
        rows = pl.ds(pl.multiple_of(b * NTOK, NTOK), NTOK)
        key = jnp.sum(jnp.where(colid == b, smcol[...], 0), axis=1, keepdims=True)
        ef = dot(onehot(key == zlane), arr[...])
        e = ef.astype(BF)
        wsum[...] += dot_t(cb[rows, :], e)
        pj = dot(proj_t[...], e).astype(BF)
        for i in range(4):
            bdp[i * RANK : (i + 1) * RANK, i * 256 : (i + 1) * 256] = pj
        ep = dot(q_fm, e).astype(BF)
        ecat = jnp.concatenate([ep[i * 64 : (i + 1) * 64] for i in range(4)], 1)
        x = dot_t(ecat, bdp[...])
        mean = jnp.sum(x, keepdims=True) / (NTOK * RANK)
        xc = x - mean
        var = jnp.sum(xc * xc, keepdims=True) / (NTOK * RANK)
        xn = xc * lax.rsqrt(var + 1e-05)
        for i in range(3):
            fplane[i, pl.ds(pl.multiple_of(b * 64, 64), 64), :] = xn[:, i * 128 : (i + 1) * 128]
        ra, rb = pltpu.roll(ef[:, 0:128], 64, 1), pltpu.roll(ef[:, 128:256], 64, 1)
        bdc[0:256, 0:256] = e
        bdc[256:512, 128:256] = jnp.where(low, 0.0, ra).astype(BF)
        bdc[256:512, 256:384] = jnp.where(low, ra, rb).astype(BF)
        y = dot(weo[...], bdc[...])
        for i in range(3):
            mplane[i, pl.ds(pl.multiple_of(b * 128, 128), 128), :] = y[:, i * 128 : (i + 1) * 128]
        return carry

    lax.fori_loop(0, B, forward, 0)

    def wtile_at(ref, p):
        return ref.at[pl.ds(pl.multiple_of((p // 2) * 8, 8), 8), pl.ds(pl.multiple_of(lax.rem(p, 2) * 128, 128), 128)]

    wrecv[me] = wtile_at(wsum, me)[...]
    plane_send(lambda p: wtile_at(wsum, p), wrecv.at[me], s_w)

    wait(zrecv.at[pl.ds(0, NZ - 1)], s_z.at[1])
    zrecv[z] = jnp.zeros((16, ROWS), BF)
    acc = tgf[z]
    for i in range(NZ):
        acc = acc + zrecv[i].astype(F32)
    zfull[z] = acc

    def ring(s, way):
        k = 2 * s + way
        if way == 0:
            c, to = lax.rem(z - s + NZ, NZ), lax.rem(z + 1, NZ)
        else:
            c, to = lax.rem(z + s, NZ), lax.rem(z + NZ - 1, NZ)
        return pltpu.make_async_remote_copy(
            src_ref=zfull.at[c], dst_ref=zfull.at[c], send_sem=s_gs.at[k], recv_sem=s_gr.at[k],
            device_id={"dp": to}, device_id_type=MESH,
        )

    def ring_recv(s, way):
        c = lax.rem(z - s - 1 + NZ, NZ) if way == 0 else lax.rem(z + s + 1, NZ)
        pltpu.make_async_copy(zfull.at[c], zfull.at[c], s_gr.at[2 * s + way]).wait()

    ring(0, 0).start()
    ring(0, 1).start()

    def out_fm(q, carry):
        for i in range(3):
            at = pl.multiple_of(q * 384 + i * 128, 128)
            fm_o[:, pl.ds(at, 128)] = fplane[i, pl.ds(q, B, stride=64), :].astype(BF)
        return carry

    lax.fori_loop(0, 64, out_fm, 0, unroll=8)

    def out_comp(q, carry):
        for i in range(3):
            at = pl.multiple_of(q * 384 + i * 128, 128)
            comp_o[:, pl.ds(at, 128)] = mplane[i, pl.ds(q, B, stride=128), :].astype(BF)
        return carry

    lax.fori_loop(0, 128, out_comp, 0, unroll=8)

    wait(wrecv.at[pl.ds(0, NP - 1)], s_w.at[1])
    wtile[...] = jnp.sum(wrecv[...], axis=0)
    wzrecv[z] = wtile[...]
    z_send(lambda p: wtile, wzrecv.at[z], s_wz)

    ring_recv(0, 0)
    ring(1, 0).start()
    ring_recv(0, 1)
    ring(1, 1).start()

    wait(wzrecv.at[pl.ds(0, NZ - 1)], s_wz.at[1])
    wfin[...] = jnp.sum(wzrecv[...], axis=0) / SAMPLES
    wtile_at(wfull, me)[...] = wfin[...]
    plane_send(lambda p: wfin, wtile_at(wfull, me), s_wg)

    for s in range(1, 6):
        ring_recv(s, 0)
        if s < 5:
            ring(s + 1, 0).start()
            ring_recv(s, 1)
            if s < 4:
                ring(s + 1, 1).start()
    tg_o[...] = zfull[...].reshape(D, ROWS)

    wait(wrecv.at[pl.ds(0, NP - 1)], s_wg.at[1])
    wg_o[...] = wfull[...]

    wait(reqs.at[pl.ds(0, NP - 1)], s_rq.at[0])
    wait(bsend.at[pl.ds(0, NP - 1)], s_b.at[0])
    wait(asend.at[pl.ds(0, NP - 1)], s_a.at[0])
    wait(zsend.at[pl.ds(0, NZ - 1)], s_z.at[0])
    wait(wrecv.at[pl.ds(0, NP - 1)], s_w.at[0])
    wait(wzrecv.at[pl.ds(0, NZ - 1)], s_wz.at[0])
    wait(wrecv.at[pl.ds(0, NP - 1)], s_wg.at[0])
    for s in range(6):
        ring(s, 0).wait_send()
        if s < 5:
            ring(s, 1).wait_send()


def on_device(emb_table, requests, token_slot, kept_mask, fm_proj, comp_weight, comp_cotangent):
    vm = pl.BlockSpec(memory_space=pltpu.VMEM)
    v = pltpu.VMEM
    dma2 = pltpu.SemaphoreType.DMA((2,))
    fm, comp, tg_t, wg = pl.pallas_call(
        kernel,
        out_shape=(
            jax.ShapeDtypeStruct((B, NTOK * RANK), BF),
            jax.ShapeDtypeStruct((B, NCOMP * D), BF),
            jax.ShapeDtypeStruct((D, ROWS), F32),
            jax.ShapeDtypeStruct((NCOMP, NTOK), F32),
        ),
        in_specs=[vm] * 7,
        out_specs=(vm,) * 4,
        scratch_shapes=[
            v((NP, 1, 128), jnp.int32), v((NP, 1, 128), jnp.int32),
            v((16, 128), jnp.int32), v((16, 128, 128), jnp.int32),
            v((B, NTOK), jnp.int32), v((NTOK, 128), jnp.int32),
            v((2, TOK, 128), F32), v((TOK, 256), BF), v((TOK, 256), BF),
            v((ROWS, 256), BF), v((256, 256), BF),
            v((NP, PACK, 128), BF), v((NP, PACK, 128), BF),
            v((NP, PACK, 128), BF), v((NP, PACK, 128), BF),
            v((TOK, 256), BF), v((TOK, 256), BF),
            v((NZ, 16, ROWS), F32), v((NZ, 16, ROWS), BF),
            v((NZ, 16, ROWS), BF), v((NZ, 16, ROWS), F32),
            v((128, 512), BF), v((384, 1024), BF), v((512, 384), BF),
            v((3, 512, 128), F32), v((3, 1024, 128), F32),
            v((256, 256), F32), v((NP, 8, 128), F32), v((8, 128), F32),
            v((NZ, 8, 128), F32), v((8, 128), F32), v((256, 256), F32),
            dma2, dma2, dma2, dma2, dma2, dma2, dma2,
            pltpu.SemaphoreType.DMA((12,)), pltpu.SemaphoreType.DMA((12,)),
        ],
        compiler_params=pltpu.CompilerParams(
            collective_id=0, has_side_effects=True, vmem_limit_bytes=48 * 1024 * 1024
        ),
    )(
        emb_table.T, requests[0].T, token_slot, kept_mask, fm_proj.T, comp_weight, comp_cotangent
    )
    return fm, comp, tg_t.T, wg


def solution(mesh):
    return jax.shard_map(
        on_device,
        mesh=mesh,
        in_specs=(
            P("emb", None),
            P(("dp", "emb"), None, None),
            P(("dp", "emb"), None),
            P(("dp", "emb"), None),
            P(),
            P(),
            P(("dp", "emb"), None),
        ),
        out_specs=(P(("dp", "emb"), None), P(("dp", "emb"), None), P("emb", None), P()),
        check_vma=False,
    )
```

```python
import functools

import jax
import jax.numpy as jnp
from jax import lax
from jax.experimental import pallas as pl
from jax.experimental.pallas import tpu as pltpu
from jax.sharding import PartitionSpec as P

MESH = pl.DeviceIdType.MESH
BF = jnp.bfloat16
F32 = jnp.float32
NZ, NY, NX, NC = 12, 8, 4, 2
NP = NY * NX * NC
D, NTOK, RANK, NCOMP, B, ROWS, CAP = 192, 256, 96, 256, 8, 1024, 32
TOK = B * NTOK
PACK = CAP + CAP // 2
SAMPLES = 6144


def dot(a, b):
    return jnp.dot(a, b, preferred_element_type=F32)


def dot_t(a, b):
    return lax.dot_general(a, b, (((1,), (1,)), ((), ())), preferred_element_type=F32)


def onehot(mask):
    return mask.astype(F32).astype(BF)


def alternate(e, n):
    half = (e + 1) // 2
    return lax.rem(jnp.where(lax.rem(e, 2) == 1, half, n - half), n)


def far_first(e):
    return alternate(15 - e, 16)


def kernel(
    table_h, req_h, slot_h, mask_h, proj_h, weight_h, cot_h,
    fm_h, comp_h, tg_h, wg_h,
    fm_o, comp_o,
    table_t, req_t, slot, mask, proj_t, weight, cot,
    reqs, reqm, reqr, wrow, wcol, slot8, keyb, pq,
    cplane, cb, rg, table, wt,
    bsend, brecv, asend, arecv, ret, arr,
    tgf, zsend, zrecv, zfull,
    eb, weo, bdp, bdc, fplane, mplane,
    wsum, wb, w1, wpart, w2, wtile, wzrecv, wquart, wq, wfull, wg_o, tg_o,
    s_in, s_rq, s_rq2, s_b, s_as, s_ar, s_z, s_w1, s_w2, s_wz, s_w4, s_w5, s_gs, s_gr, s_out,
):
    loads = [
        pltpu.make_async_copy(src, dst, s_in.at[i])
        for i, (src, dst) in enumerate([
            (req_h, req_t), (slot_h, slot), (mask_h, mask), (cot_h, cot),
            (weight_h, weight), (table_h, table_t), (proj_h, proj_t),
        ])
    ]
    for load in loads:
        load.start()
    z = lax.axis_index("dp")
    me = lax.axis_index("emb")
    my = me // (NX * NC)
    mx = lax.rem(me // NC, NX)
    mc = lax.rem(me, NC)

    def peer(j):
        dy = alternate(lax.rem(j, NY), NY)
        dxc = j // NY
        py = lax.rem(my + dy, NY)
        px = lax.rem(mx + dxc // NC, NX)
        pc = lax.rem(mc + dxc, NC)
        return (py * NX + px) * NC + pc

    def zpeer(j):
        return lax.rem(z + alternate(j, NZ), NZ)

    def wait(ref, sem):
        pltpu.make_async_copy(ref, ref, sem).wait()

    mxc = lax.rem(me, NX * NC)

    def row_peer(k):
        return lax.rem(mxc + k, NX * NC)

    def row_send(src, dst, sems):
        for k in range(1, NX * NC):
            xc = row_peer(k)
            pltpu.make_async_remote_copy(
                src_ref=src(xc), dst_ref=dst, send_sem=sems.at[0], recv_sem=sems.at[1],
                device_id={"emb": my * NX * NC + xc}, device_id_type=MESH,
            ).start()

    def column_send(src, dst, sems):
        for k in range(1, NY):
            y = lax.rem(my + alternate(jnp.int32(k), NY), NY)
            pltpu.make_async_remote_copy(
                src_ref=src(y), dst_ref=dst, send_sem=sems.at[0], recv_sem=sems.at[1],
                device_id={"emb": y * NX * NC + mxc}, device_id_type=MESH,
            ).start()

    def z_send(src, dst, sems):
        def body(j, carry):
            p = zpeer(j)
            pltpu.make_async_remote_copy(
                src_ref=src(p), dst_ref=dst, send_sem=sems.at[0], recv_sem=sems.at[1],
                device_id={"dp": p}, device_id_type=MESH,
            ).start()
            return carry
        lax.fori_loop(1, NZ, body, 0)

    barrier = pltpu.get_barrier_semaphore()

    def sig_plane(j, carry):
        pl.semaphore_signal(barrier, inc=1, device_id={"emb": peer(j)}, device_id_type=MESH)
        return carry

    def sig_z(j, carry):
        pl.semaphore_signal(barrier, inc=1, device_id={"dp": zpeer(j)}, device_id_type=MESH)
        return carry

    lax.fori_loop(1, NP, sig_plane, 0, unroll=3)
    lax.fori_loop(1, NZ, sig_z, 0)

    lane = lax.broadcasted_iota(jnp.int32, (1, 128), 1)
    low = lane < 64

    for load in loads[:3]:
        load.wait()

    rt = jnp.concatenate([req_t[...], jnp.zeros((128 - CAP, NP), jnp.int32)], 0)
    rt = jnp.concatenate([rt, jnp.zeros((128, 128 - NP), jnp.int32)], 1).T
    rt = rt[0:NP]
    tiled = rt
    for i in range(1, 4):
        tiled = tiled + pltpu.roll(rt, 32 * i, 1)
    tiled = jnp.where(lane // CAP == lax.rem(me, 4), tiled, 0)
    for p in range(NP):
        reqs[p % 8, p // 8] = tiled[p : p + 1]

    for b in range(B):
        slot8[b : b + 1, :] = slot[0:1, b * NTOK : (b + 1) * NTOK]
    masked = jnp.where(mask[...] > 0, slot8[...], -1)
    slot8[...] = masked

    loads[3].wait()
    loads[4].wait()

    def unpack_cot(mp, carry):
        at = pl.multiple_of(mp * 384, 128)
        x = cot[:, pl.ds(at, 384)].astype(F32)
        x0, x1, x2 = x[:, 0:128], x[:, 128:256], x[:, 256:384]
        r1 = pltpu.roll(x1, 64, 1)
        r2 = pltpu.roll(x2, 64, 1)
        ev, od = pl.ds(2 * mp, B, stride=NCOMP), pl.ds(2 * mp + 1, B, stride=NCOMP)
        cplane[0, ev, :] = x0
        cplane[1, ev, :] = jnp.where(low, x1, r1)
        cplane[0, od, :] = jnp.where(low, r1, r2)
        cplane[1, od, :] = jnp.where(low, r2, x2)
        return carry

    lax.fori_loop(0, NCOMP // 2, unpack_cot, 0, unroll=8)
    wt[...] = weight[...].astype(F32).T.astype(BF)

    def make_rg(b, carry):
        rows = pl.ds(pl.multiple_of(b * NCOMP, NCOMP), NCOMP)
        c = jnp.concatenate([cplane[0, rows, :], cplane[1, rows, :]], 1).astype(BF)
        cb[rows, :] = c
        rg[rows, :] = dot(wt[...], c).astype(BF)
        return carry

    lax.fori_loop(0, B, make_rg, 0)

    pl.semaphore_wait(barrier, NP - 1 + NZ - 1)
    reqm[:, mxc] = reqs[mxc]
    row_send(lambda xc: reqs.at[xc], reqm.at[:, mxc], s_rq)

    sub = lax.broadcasted_iota(jnp.int32, (128, 1), 0)

    def send4(buf, dst, g, send_sem, recv_sem):
        for q in range(4):
            p = g * 4 + lax.rem(me + q, 4)

            @pl.when(p != me)
            def _():
                pltpu.make_async_remote_copy(
                    src_ref=buf.at[p], dst_ref=dst, send_sem=send_sem, recv_sem=recv_sem,
                    device_id={"emb": p}, device_id_type=MESH,
                ).start()

    def packed(val, dst, g):
        for q in range(4):
            v = val[q * CAP : (q + 1) * CAP]
            dst[g * 4 + q, 0:CAP, :] = v[:, 0:128].astype(BF)
            dst[g * 4 + q, CAP:PACK, :] = jnp.where(low, v[0:16, 128:256], v[16:32, 128:256]).astype(BF)

    def order(e, carry):
        g = lax.rem(me // 4 + far_first(e), 16)
        key = sub + g * 128
        pt = jnp.concatenate([onehot(slot8[b : b + 1, :] == key) for b in range(B)], 1)
        packed(dot(pt, rg[...]), bsend, g)
        send4(bsend, brecv.at[me], g, s_b.at[0], s_b.at[1])
        return carry

    lax.fori_loop(0, 6, order, 0)
    wait(reqs.at[pl.ds(0, 7)], s_rq.at[1])
    reqr[my] = reqm[my]
    column_send(lambda y: reqm.at[y], reqr.at[my], s_rq2)
    lax.fori_loop(6, 16, order, 0)
    brecv[me] = bsend[me]

    loads[5].wait()
    for i in range(8):
        blk = table_t[:, i * 128 : (i + 1) * 128].astype(F32)
        blk = jnp.concatenate([blk, blk[128:192]], 0).T
        table[i * 128 : (i + 1) * 128, :] = blk.astype(BF)

    wait(reqr.at[pl.ds(0, 7)], s_rq2.at[1])
    for g in range(16):
        y, h = g // 2, (g % 2) * 4
        wrow[g : g + 1, :] = reqr[y, h] + reqr[y, h + 1] + reqr[y, h + 2] + reqr[y, h + 3]
    wc = jnp.concatenate([wrow[...], jnp.zeros((112, 128), jnp.int32)], 0).T
    for g in range(16):
        wcol[g] = jnp.broadcast_to(wc[:, g : g + 1], (128, 128))
    rlane = lax.broadcasted_iota(jnp.int32, (1, 128), 1)

    def fetch(e, carry):
        g = lax.rem(me // 4 + far_first(e), 16)
        col = wcol[g]
        o = jnp.concatenate([onehot(col == rlane + 128 * i) for i in range(8)], 1)
        packed(dot(o, table[...]), asend, g)
        send4(asend, arecv.at[me], g, s_as, s_ar.at[e // 4])
        return carry

    lax.fori_loop(0, 16, fetch, 0)
    arecv[me] = asend[me]

    def group_from(e):
        return lax.rem(me // 4 - far_first(e) + 16, 16)

    km = jnp.concatenate([slot8[...], jnp.full((120, NTOK), -1, jnp.int32)], 0).T
    for b in range(B):
        keyb[b] = jnp.broadcast_to(km[:, b : b + 1], (NTOK, 128))

    def choose(k, carry):
        q, b = k // B, lax.rem(k, B)
        key = keyb[b]
        o = [onehot(key == rlane + 128 * group_from(4 * q + i)) for i in range(4)]
        pq[q, pl.ds(pl.multiple_of(b * NTOK, NTOK), NTOK), :] = jnp.concatenate(o, 1)
        return carry

    lax.fori_loop(0, 4 * B, choose, 0)

    def unpack_one(src, p, dst, at):
        dst[pl.ds(at, CAP), 0:128] = src[p, 0:CAP, :]
        h = src[p, CAP:PACK, :].astype(F32)
        dst[pl.ds(at, 16), 128:256] = jnp.where(low, h, 0.0).astype(BF)
        h = pltpu.roll(h, 64, 1)
        dst[pl.ds(pl.multiple_of(at + 16, 16), 16), 128:256] = jnp.where(low, h, 0.0).astype(BF)

    wait(brecv.at[pl.ds(0, NP - 1)], s_b.at[1])

    def unpack_ret(p, carry):
        unpack_one(brecv, p, ret, pl.multiple_of(p * CAP, CAP))
        return carry

    lax.fori_loop(0, NP, unpack_ret, 0, unroll=4)

    def scatter(rb, carry):
        key = sub + rb * 128
        o = jnp.concatenate([onehot(wrow[g : g + 1, :] == key) for g in range(16)], 1)
        t = dot(o, ret[...])
        t = t.T[0:D].reshape(NZ, 16, 128)
        at = pl.ds(pl.multiple_of(rb * 128, 128), 128)
        tgf[:, :, at] = t
        zsend[:, :, at] = t.astype(BF)
        return carry

    lax.fori_loop(0, 8, scatter, 0)
    z_send(lambda p: zsend.at[p], zrecv.at[z], s_z)

    def zpart(c):
        return zfull.at[pl.ds(pl.multiple_of(lax.rem(c + NZ, NZ) * 16, 16), 16)]

    steps = [
        (0, 6), (0, 3), (0, -3), (0, 1), (0, -1),
        (-3, 1), (-3, -1), (3, 1), (3, -1), (6, 1), (6, -1),
    ]

    def hand(k):
        a, d = steps[k]
        return pltpu.make_async_remote_copy(
            src_ref=zpart(z + a), dst_ref=zpart(z + a), send_sem=s_gs.at[k], recv_sem=s_gr.at[k],
            device_id={"dp": lax.rem(z + d + NZ, NZ)}, device_id_type=MESH,
        )

    def got(k):
        a, d = steps[k]
        wait(zpart(z - d + a), s_gr.at[k])

    def sum_z():
        wait(zrecv.at[pl.ds(0, NZ - 1)], s_z.at[1])
        zrecv[z] = jnp.zeros((16, ROWS), BF)
        acc = tgf[z]
        for i in range(NZ):
            acc = acc + zrecv[i].astype(F32)
        zpart(z)[...] = acc.astype(BF)
        for k in range(5):
            hand(k).start()

    r256 = lax.broadcasted_iota(jnp.int32, (256, 256), 0)
    c256 = lax.broadcasted_iota(jnp.int32, (256, 256), 1)
    q_fm = onehot(c256 == 4 * lax.rem(r256, 64) + r256 // 64)
    q_w = onehot(c256 == 2 * lax.rem(r256, 128) + r256 // 128)
    wp = dot(q_w, weight[...]).astype(BF)
    weo[...] = jnp.concatenate([wp[0:128], wp[128:256]], 1)
    bdp[...] = jnp.zeros_like(bdp)
    bdc[...] = jnp.zeros_like(bdc)
    loads[6].wait()
    wsum[...] = jnp.zeros_like(wsum)

    def batch_rows(b):
        return pl.ds(pl.multiple_of(b * NTOK, NTOK), NTOK)

    for q in range(4):
        wait(arecv.at[pl.ds(0, 15 if q == 3 else 16)], s_ar.at[q])

        def unpack_arr(k, carry):
            i, c = k // 4, lax.rem(k, 4)
            unpack_one(arecv, group_from(4 * q + i) * 4 + c, arr, pl.multiple_of(k * CAP, CAP))
            return carry

        lax.fori_loop(0, 16, unpack_arr, 0, unroll=4)

        def embed(b, carry):
            rows = batch_rows(b)
            e = dot(pq[q, rows, :], arr[...])
            if q > 0:
                e = e + eb[rows, :].astype(F32)
            e = e.astype(BF)
            eb[rows, :] = e
            if q == 3:
                wsum[...] += dot_t(cb[rows, :], e)
            return carry

        lax.fori_loop(0, B, embed, 0)

    def slab(ref, xc):
        return ref.at[pl.ds(pl.multiple_of(xc * 32, 32), 32)]

    def tile(ref, y):
        return ref.at[pl.ds(pl.multiple_of((y // 2) * 8, 8), 8), pl.ds(pl.multiple_of(lax.rem(y, 2) * 128, 128), 128)]

    wb[...] = wsum[...].astype(BF)
    w1[mxc] = slab(wb, mxc)[...]
    row_send(lambda xc: slab(wb, xc), w1.at[mxc], s_w1)
    sum_z()

    def forward(b, carry):
        e = eb[batch_rows(b), :]
        ef = e.astype(F32)
        pj = dot(proj_t[...], e).astype(BF)
        for i in range(4):
            bdp[i * RANK : (i + 1) * RANK, i * 256 : (i + 1) * 256] = pj
        ep = dot(q_fm, e).astype(BF)
        ecat = jnp.concatenate([ep[i * 64 : (i + 1) * 64] for i in range(4)], 1)
        x = dot_t(ecat, bdp[...])
        mean = jnp.sum(x, keepdims=True) / (NTOK * RANK)
        xc = x - mean
        var = jnp.sum(xc * xc, keepdims=True) / (NTOK * RANK)
        xn = xc * lax.rsqrt(var + 1e-05)
        for i in range(3):
            fplane[i, pl.ds(pl.multiple_of(b * 64, 64), 64), :] = xn[:, i * 128 : (i + 1) * 128]
        ra, rb = pltpu.roll(ef[:, 0:128], 64, 1), pltpu.roll(ef[:, 128:256], 64, 1)
        bdc[0:256, 0:256] = e
        bdc[256:512, 128:256] = jnp.where(low, 0.0, ra).astype(BF)
        bdc[256:512, 256:384] = jnp.where(low, ra, rb).astype(BF)
        y = dot(weo[...], bdc[...])
        for i in range(3):
            mplane[i, pl.ds(pl.multiple_of(b * 128, 128), 128), :] = y[:, i * 128 : (i + 1) * 128]
        return carry

    lax.fori_loop(0, 3, forward, 0)
    wait(w1.at[pl.ds(0, 7)], s_w1.at[1])
    wpart[...] = jnp.sum(w1[...].astype(F32), axis=0)
    w2[my] = tile(wpart, my)[...]
    column_send(lambda y: tile(wpart, y), w2.at[my], s_w2)
    got(1)
    hand(5).start()
    hand(6).start()
    got(2)
    hand(7).start()
    hand(8).start()
    wait(w2.at[pl.ds(0, 7)], s_w2.at[1])
    wtile[...] = jnp.sum(w2[...], axis=0)
    wzrecv[z] = wtile[...]
    z_send(lambda p: wtile, wzrecv.at[z], s_wz)
    got(0)
    hand(9).start()
    hand(10).start()
    lax.fori_loop(3, 6, forward, 0)
    wait(wzrecv.at[pl.ds(0, NZ - 1)], s_wz.at[1])
    tile(wquart, my)[...] = jnp.sum(wzrecv[...], axis=0) / SAMPLES
    column_send(lambda y: tile(wquart, my), tile(wquart, my), s_w4)
    lax.fori_loop(6, B, forward, 0)

    def out_fm(q, carry):
        for i in range(3):
            at = pl.multiple_of(q * 384 + i * 128, 128)
            fm_o[:, pl.ds(at, 128)] = fplane[i, pl.ds(q, B, stride=64), :].astype(BF)
        return carry

    lax.fori_loop(0, 64, out_fm, 0, unroll=8)

    store_fm = pltpu.make_async_copy(fm_o, fm_h, s_out.at[0])
    store_fm.start()
    wait(w2.at[pl.ds(0, 7)], s_w4.at[1])
    wq[...] = wquart[...].astype(BF)
    slab(wfull, mxc)[...] = wq[...]
    row_send(lambda xc: wq, slab(wfull, mxc), s_w5)

    def out_comp(q, carry):
        for i in range(3):
            at = pl.multiple_of(q * 384 + i * 128, 128)
            comp_o[:, pl.ds(at, 128)] = mplane[i, pl.ds(q, B, stride=128), :].astype(BF)
        return carry

    lax.fori_loop(0, 128, out_comp, 0, unroll=8)

    store_comp = pltpu.make_async_copy(comp_o, comp_h, s_out.at[1])
    store_comp.start()
    for k in range(3, 11):
        got(k)
    tg_o[...] = zfull[...].astype(F32)
    store_tg = pltpu.make_async_copy(tg_o, tg_h, s_out.at[2])
    store_tg.start()
    wait(w1.at[pl.ds(0, 7)], s_w5.at[1])
    wg_o[...] = wfull[...].astype(F32)
    store_wg = pltpu.make_async_copy(wg_o, wg_h, s_out.at[3])
    store_wg.start()

    wait(reqs.at[pl.ds(0, 7)], s_rq.at[0])
    wait(reqr.at[pl.ds(0, 7)], s_rq2.at[0])
    wait(bsend.at[pl.ds(0, NP - 1)], s_b.at[0])
    wait(asend.at[pl.ds(0, NP - 1)], s_as)
    wait(zsend.at[pl.ds(0, NZ - 1)], s_z.at[0])
    wait(w1.at[pl.ds(0, 7)], s_w1.at[0])
    wait(w2.at[pl.ds(0, 7)], s_w2.at[0])
    wait(wzrecv.at[pl.ds(0, NZ - 1)], s_wz.at[0])
    wait(w2.at[pl.ds(0, 7)], s_w4.at[0])
    wait(w1.at[pl.ds(0, 7)], s_w5.at[0])
    for k in range(11):
        hand(k).wait_send()
    store_fm.wait()
    store_comp.wait()
    store_tg.wait()
    store_wg.wait()


def deliver(fm_i, comp_i, tg_i, wg_i, fm_o, comp_o, tg_o, wg_o, fm_v, comp_v, tg_v, wg_v, sems):
    held = [(comp_i, comp_v, comp_o), (tg_i, tg_v, tg_o), (fm_i, fm_v, fm_o), (wg_i, wg_v, wg_o)]
    loads = [pltpu.make_async_copy(src, mid, sems.at[0, i]) for i, (src, mid, _) in enumerate(held)]
    stores = [pltpu.make_async_copy(mid, dst, sems.at[1, i]) for i, (_, mid, dst) in enumerate(held)]
    for load in loads:
        load.start()
    for load, store in zip(loads, stores):
        load.wait()
        store.start()
    for store in stores:
        store.wait()


def on_device(emb_table, requests, token_slot, kept_mask, fm_proj, comp_weight, comp_cotangent):
    shapes = (
        jax.ShapeDtypeStruct((B, NTOK * RANK), BF),
        jax.ShapeDtypeStruct((B, NCOMP * D), BF),
        jax.ShapeDtypeStruct((D, ROWS), F32),
        jax.ShapeDtypeStruct((NCOMP, NTOK), F32),
    )
    hbm = pl.BlockSpec(memory_space=pl.ANY)
    v = pltpu.VMEM
    dma2 = pltpu.SemaphoreType.DMA((2,))
    outs = pl.pallas_call(
        kernel,
        out_shape=shapes,
        in_specs=[hbm] * 7,
        out_specs=(hbm,) * 4,
        scratch_shapes=[
            v((B, NTOK * RANK), BF), v((B, NCOMP * D), BF),
            v((D, ROWS), BF), v((CAP, NP), jnp.int32), v((1, TOK), jnp.int32), v((B, NTOK), jnp.int32),
            v((RANK, NTOK), BF), v((NCOMP, NTOK), BF), v((B, NCOMP * D), BF),
            v((8, 8, 1, 128), jnp.int32), v((8, 8, 1, 128), jnp.int32), v((8, 8, 1, 128), jnp.int32),
            v((16, 128), jnp.int32), v((16, 128, 128), jnp.int32),
            v((B, NTOK), jnp.int32), v((B, NTOK, 128), jnp.int32), v((4, TOK, 512), BF),
            v((2, TOK, 128), F32), v((TOK, 256), BF), v((TOK, 256), BF),
            v((ROWS, 256), BF), v((256, 256), BF),
            v((NP, PACK, 128), BF), v((NP, PACK, 128), BF),
            v((NP, PACK, 128), BF), v((NP, PACK, 128), BF),
            v((TOK, 256), BF), v((512, 256), BF),
            v((NZ, 16, ROWS), F32), v((NZ, 16, ROWS), BF),
            v((NZ, 16, ROWS), BF), v((D, ROWS), BF),
            v((TOK, 256), BF), v((128, 512), BF), v((384, 1024), BF), v((512, 384), BF),
            v((3, 512, 128), F32), v((3, 1024, 128), F32),
            v((256, 256), F32), v((256, 256), BF), v((8, 32, 256), BF), v((32, 256), F32), v((8, 8, 128), F32),
            v((8, 128), F32), v((NZ, 8, 128), F32), v((32, 256), F32), v((32, 256), BF), v((256, 256), BF),
            v((NCOMP, NTOK), F32), v((D, ROWS), F32),
            pltpu.SemaphoreType.DMA((7,)), dma2, dma2, dma2, pltpu.SemaphoreType.DMA, pltpu.SemaphoreType.DMA((4,)),
            dma2, dma2, dma2, dma2, dma2, dma2,
            pltpu.SemaphoreType.DMA((12,)), pltpu.SemaphoreType.DMA((12,)), pltpu.SemaphoreType.DMA((4,)),
        ],
        compiler_params=pltpu.CompilerParams(
            collective_id=0, has_side_effects=True, vmem_limit_bytes=62 * 1024 * 1024
        ),
    )(
        emb_table.T, requests[0].T, token_slot, kept_mask, fm_proj.T, comp_weight, comp_cotangent
    )
    fm, comp, tg_t, wg = pl.pallas_call(
        deliver,
        out_shape=shapes,
        in_specs=[hbm] * 4,
        out_specs=(hbm,) * 4,
        scratch_shapes=[v(x.shape, x.dtype) for x in shapes] + [pltpu.SemaphoreType.DMA((2, 4))],
        compiler_params=pltpu.CompilerParams(vmem_limit_bytes=62 * 1024 * 1024),
    )(*outs)
    return fm, comp, tg_t.T, wg


def solution(mesh):
    return jax.shard_map(
        on_device,
        mesh=mesh,
        in_specs=(
            P("emb", None),
            P(("dp", "emb"), None, None),
            P(("dp", "emb"), None),
            P(("dp", "emb"), None),
            P(),
            P(),
            P(("dp", "emb"), None),
        ),
        out_specs=(P(("dp", "emb"), None), P(("dp", "emb"), None), P("emb", None), P()),
        check_vma=False,
    )
```

```python
import functools

import jax
import jax.numpy as jnp
from jax import lax
from jax.experimental import pallas as pl
from jax.experimental.pallas import tpu as pltpu
from jax.sharding import PartitionSpec as P

MESH = pl.DeviceIdType.MESH
BF = jnp.bfloat16
F32 = jnp.float32
NZ, NY, NX, NC = 12, 8, 4, 2
NP = NY * NX * NC
D, NTOK, RANK, NCOMP, B, ROWS, CAP = 192, 256, 96, 256, 8, 1024, 32
TOK = B * NTOK
PACK = CAP + CAP // 2
SAMPLES = 6144


def dot(a, b):
    return jnp.dot(a, b, preferred_element_type=F32)


def dot_t(a, b):
    return lax.dot_general(a, b, (((1,), (1,)), ((), ())), preferred_element_type=F32)


def onehot(mask):
    return mask.astype(F32).astype(BF)


def alternate(e, n):
    half = (e + 1) // 2
    return lax.rem(jnp.where(lax.rem(e, 2) == 1, half, n - half), n)


def far_first(e):
    return alternate(15 - e, 16)


def kernel(
    table_h, req_h, slot_h, mask_h, proj_h, weight_h, cot_h,
    fm_h, comp_h, tg_h, wg_h,
    fm_o, comp_o,
    table_t, req_t, slot, mask, proj_t, weight, cot,
    reqs, reqm, reqr, wrow, wcol, slot8, keyb, pq,
    cplane, cb, rg, table, wt,
    bsend, brecv, asend, arecv, ret, arr,
    tgf, zsend, zrecv, zfull,
    eb, weo, bdp, bdc, fplane, mplane,
    wsum, wb, w1, wpart, w2, wtile, wzrecv, wquart, wq, wfull, wg_o, tg_o,
    s_in, s_rq, s_rq2, s_b, s_as, s_ar, s_z, s_w1, s_w2, s_wz, s_w4, s_w5, s_gs, s_gr, s_out,
):
    loads = [
        pltpu.make_async_copy(src, dst, s_in.at[i])
        for i, (src, dst) in enumerate([
            (req_h, req_t), (slot_h, slot), (mask_h, mask), (cot_h, cot),
            (weight_h, weight), (table_h, table_t), (proj_h, proj_t),
        ])
    ]
    for load in loads:
        load.start()
    z = lax.axis_index("dp")
    me = lax.axis_index("emb")
    my = me // (NX * NC)
    mx = lax.rem(me // NC, NX)
    mc = lax.rem(me, NC)

    def peer(j):
        dy = alternate(lax.rem(j, NY), NY)
        dxc = j // NY
        py = lax.rem(my + dy, NY)
        px = lax.rem(mx + dxc // NC, NX)
        pc = lax.rem(mc + dxc, NC)
        return (py * NX + px) * NC + pc

    def zpeer(j):
        return lax.rem(z + alternate(j, NZ), NZ)

    def wait(ref, sem):
        pltpu.make_async_copy(ref, ref, sem).wait()

    mxc = lax.rem(me, NX * NC)

    def row_peer(k):
        return lax.rem(mxc + k, NX * NC)

    def row_send(src, dst, sems):
        for k in range(1, NX * NC):
            xc = row_peer(k)
            pltpu.make_async_remote_copy(
                src_ref=src(xc), dst_ref=dst, send_sem=sems.at[0], recv_sem=sems.at[1],
                device_id={"emb": my * NX * NC + xc}, device_id_type=MESH,
            ).start()

    def column_send(src, dst, sems):
        for k in range(1, NY):
            y = lax.rem(my + alternate(jnp.int32(k), NY), NY)
            pltpu.make_async_remote_copy(
                src_ref=src(y), dst_ref=dst, send_sem=sems.at[0], recv_sem=sems.at[1],
                device_id={"emb": y * NX * NC + mxc}, device_id_type=MESH,
            ).start()

    def z_send(src, dst, sems):
        def body(j, carry):
            p = zpeer(j)
            pltpu.make_async_remote_copy(
                src_ref=src(p), dst_ref=dst, send_sem=sems.at[0], recv_sem=sems.at[1],
                device_id={"dp": p}, device_id_type=MESH,
            ).start()
            return carry
        lax.fori_loop(1, NZ, body, 0)

    barrier = pltpu.get_barrier_semaphore()

    def sig_plane(j, carry):
        pl.semaphore_signal(barrier, inc=1, device_id={"emb": peer(j)}, device_id_type=MESH)
        return carry

    def sig_z(j, carry):
        pl.semaphore_signal(barrier, inc=1, device_id={"dp": zpeer(j)}, device_id_type=MESH)
        return carry

    lax.fori_loop(1, NP, sig_plane, 0, unroll=3)
    lax.fori_loop(1, NZ, sig_z, 0)

    lane = lax.broadcasted_iota(jnp.int32, (1, 128), 1)
    low = lane < 64

    for load in loads[:3]:
        load.wait()

    rt = jnp.concatenate([req_t[...], jnp.zeros((128 - CAP, NP), jnp.int32)], 0)
    rt = jnp.concatenate([rt, jnp.zeros((128, 128 - NP), jnp.int32)], 1).T
    rt = rt[0:NP]
    tiled = rt
    for i in range(1, 4):
        tiled = tiled + pltpu.roll(rt, 32 * i, 1)
    tiled = jnp.where(lane // CAP == lax.rem(me, 4), tiled, 0)
    for p in range(NP):
        reqs[p % 8, p // 8] = tiled[p : p + 1]

    for b in range(B):
        slot8[b : b + 1, :] = slot[0:1, b * NTOK : (b + 1) * NTOK]
    masked = jnp.where(mask[...] > 0, slot8[...], -1)
    slot8[...] = masked

    loads[3].wait()
    loads[4].wait()

    def unpack_cot(mp, carry):
        at = pl.multiple_of(mp * 384, 128)
        x = cot[:, pl.ds(at, 384)].astype(F32)
        x0, x1, x2 = x[:, 0:128], x[:, 128:256], x[:, 256:384]
        r1 = pltpu.roll(x1, 64, 1)
        r2 = pltpu.roll(x2, 64, 1)
        ev, od = pl.ds(2 * mp, B, stride=NCOMP), pl.ds(2 * mp + 1, B, stride=NCOMP)
        cplane[0, ev, :] = x0
        cplane[1, ev, :] = jnp.where(low, x1, r1)
        cplane[0, od, :] = jnp.where(low, r1, r2)
        cplane[1, od, :] = jnp.where(low, r2, x2)
        return carry

    lax.fori_loop(0, NCOMP // 2, unpack_cot, 0, unroll=8)
    wt[...] = weight[...].astype(F32).T.astype(BF)

    def make_rg(b, carry):
        rows = pl.ds(pl.multiple_of(b * NCOMP, NCOMP), NCOMP)
        c = jnp.concatenate([cplane[0, rows, :], cplane[1, rows, :]], 1).astype(BF)
        cb[rows, :] = c
        rg[rows, :] = dot(wt[...], c).astype(BF)
        return carry

    lax.fori_loop(0, B, make_rg, 0)

    pl.semaphore_wait(barrier, NP - 1 + NZ - 1)
    reqm[:, mxc] = reqs[mxc]
    row_send(lambda xc: reqs.at[xc], reqm.at[:, mxc], s_rq)

    sub = lax.broadcasted_iota(jnp.int32, (128, 1), 0)

    def send4(buf, dst, g, send_sem, recv_sem):
        for q in range(4):
            p = g * 4 + lax.rem(me + q, 4)

            @pl.when(p != me)
            def _():
                pltpu.make_async_remote_copy(
                    src_ref=buf.at[p], dst_ref=dst, send_sem=send_sem, recv_sem=recv_sem,
                    device_id={"emb": p}, device_id_type=MESH,
                ).start()

    def packed(val, dst, g):
        for q in range(4):
            v = val[q * CAP : (q + 1) * CAP]
            dst[g * 4 + q, 0:CAP, :] = v[:, 0:128].astype(BF)
            dst[g * 4 + q, CAP:PACK, :] = jnp.where(low, v[0:16, 128:256], v[16:32, 128:256]).astype(BF)

    def order(e, carry):
        g = lax.rem(me // 4 + far_first(e), 16)
        key = sub + g * 128
        pt = jnp.concatenate([onehot(slot8[b : b + 1, :] == key) for b in range(B)], 1)
        packed(dot(pt, rg[...]), bsend, g)
        send4(bsend, brecv.at[me], g, s_b.at[0], s_b.at[1])
        return carry

    lax.fori_loop(0, 6, order, 0)
    wait(reqs.at[pl.ds(0, 7)], s_rq.at[1])
    reqr[my] = reqm[my]
    column_send(lambda y: reqm.at[y], reqr.at[my], s_rq2)
    lax.fori_loop(6, 16, order, 0)
    brecv[me] = bsend[me]

    loads[5].wait()
    for i in range(8):
        blk = table_t[:, i * 128 : (i + 1) * 128].astype(F32)
        blk = jnp.concatenate([blk, blk[128:192]], 0).T
        table[i * 128 : (i + 1) * 128, :] = blk.astype(BF)

    wait(reqr.at[pl.ds(0, 7)], s_rq2.at[1])
    for g in range(16):
        y, h = g // 2, (g % 2) * 4
        wrow[g : g + 1, :] = reqr[y, h] + reqr[y, h + 1] + reqr[y, h + 2] + reqr[y, h + 3]
    wc = jnp.concatenate([wrow[...], jnp.zeros((112, 128), jnp.int32)], 0).T
    for g in range(16):
        wcol[g] = jnp.broadcast_to(wc[:, g : g + 1], (128, 128))
    rlane = lax.broadcasted_iota(jnp.int32, (1, 128), 1)

    def fetch(e, carry):
        g = lax.rem(me // 4 + far_first(e), 16)
        col = wcol[g]
        o = jnp.concatenate([onehot(col == rlane + 128 * i) for i in range(8)], 1)
        packed(dot(o, table[...]), asend, g)
        send4(asend, arecv.at[me], g, s_as, s_ar.at[e // 4])
        return carry

    lax.fori_loop(0, 16, fetch, 0)
    arecv[me] = asend[me]

    def group_from(e):
        return lax.rem(me // 4 - far_first(e) + 16, 16)

    km = jnp.concatenate([slot8[...], jnp.full((120, NTOK), -1, jnp.int32)], 0).T
    for b in range(B):
        keyb[b] = jnp.broadcast_to(km[:, b : b + 1], (NTOK, 128))

    def choose(k, carry):
        q, b = k // B, lax.rem(k, B)
        key = keyb[b]
        o = [onehot(key == rlane + 128 * group_from(4 * q + i)) for i in range(4)]
        pq[q, pl.ds(pl.multiple_of(b * NTOK, NTOK), NTOK), :] = jnp.concatenate(o, 1)
        return carry

    lax.fori_loop(0, 4 * B, choose, 0)

    def unpack_one(src, p, dst, at):
        dst[pl.ds(at, CAP), 0:128] = src[p, 0:CAP, :]
        h = src[p, CAP:PACK, :].astype(F32)
        dst[pl.ds(at, 16), 128:256] = jnp.where(low, h, 0.0).astype(BF)
        h = pltpu.roll(h, 64, 1)
        dst[pl.ds(pl.multiple_of(at + 16, 16), 16), 128:256] = jnp.where(low, h, 0.0).astype(BF)

    wait(brecv.at[pl.ds(0, NP - 1)], s_b.at[1])

    def unpack_ret(p, carry):
        unpack_one(brecv, p, ret, pl.multiple_of(p * CAP, CAP))
        return carry

    lax.fori_loop(0, NP, unpack_ret, 0, unroll=4)

    sub2 = lax.broadcasted_iota(jnp.int32, (256, 1), 0)

    def scatter(rb, carry):
        key = sub2 + rb * 256
        o = jnp.concatenate([onehot(wrow[g : g + 1, :] == key) for g in range(16)], 1)
        t = dot(o, ret[...])
        t = t.T[0:D].reshape(NZ, 16, 256)
        at = pl.ds(pl.multiple_of(rb * 256, 256), 256)
        tgf[:, :, at] = t
        zsend[:, :, at] = t.astype(BF)
        return carry

    for h in range(2):
        lax.fori_loop(2 * h, 2 * h + 2, scatter, 0)
        half = pl.ds(512 * h, 512)
        z_send(lambda p: zsend.at[p, :, half], zrecv.at[z, :, half], s_z)

    def zpart(c):
        return zfull.at[pl.ds(pl.multiple_of(lax.rem(c + NZ, NZ) * 16, 16), 16)]

    steps = [
        (0, 6), (0, 3), (0, -3), (0, 1), (0, -1),
        (-3, 1), (-3, -1), (3, 1), (3, -1), (6, 1), (6, -1),
    ]

    def hand(k):
        a, d = steps[k]
        return pltpu.make_async_remote_copy(
            src_ref=zpart(z + a), dst_ref=zpart(z + a), send_sem=s_gs.at[k], recv_sem=s_gr.at[k],
            device_id={"dp": lax.rem(z + d + NZ, NZ)}, device_id_type=MESH,
        )

    def got(k):
        a, d = steps[k]
        wait(zpart(z - d + a), s_gr.at[k])

    def sum_z():
        wait(zrecv.at[pl.ds(0, NZ - 1)], s_z.at[1])
        zrecv[z] = jnp.zeros((16, ROWS), BF)
        acc = tgf[z]
        for i in range(NZ):
            acc = acc + zrecv[i].astype(F32)
        zpart(z)[...] = acc.astype(BF)
        for k in range(5):
            hand(k).start()

    r256 = lax.broadcasted_iota(jnp.int32, (256, 256), 0)
    c256 = lax.broadcasted_iota(jnp.int32, (256, 256), 1)
    q_fm = onehot(c256 == 4 * lax.rem(r256, 64) + r256 // 64)
    q_w = onehot(c256 == 2 * lax.rem(r256, 128) + r256 // 128)
    wp = dot(q_w, weight[...]).astype(BF)
    weo[...] = jnp.concatenate([wp[0:128], wp[128:256]], 1)
    bdp[...] = jnp.zeros_like(bdp)
    bdc[...] = jnp.zeros_like(bdc)
    loads[6].wait()
    wsum[...] = jnp.zeros_like(wsum)

    def batch_rows(b):
        return pl.ds(pl.multiple_of(b * NTOK, NTOK), NTOK)

    for q in range(4):
        wait(arecv.at[pl.ds(0, 15 if q == 3 else 16)], s_ar.at[q])

        def unpack_arr(k, carry):
            i, c = k // 4, lax.rem(k, 4)
            unpack_one(arecv, group_from(4 * q + i) * 4 + c, arr, pl.multiple_of(k * CAP, CAP))
            return carry

        lax.fori_loop(0, 16, unpack_arr, 0, unroll=4)

        def embed(b, carry):
            rows = batch_rows(b)
            e = dot(pq[q, rows, :], arr[...])
            if q > 0:
                e = e + eb[rows, :].astype(F32)
            e = e.astype(BF)
            eb[rows, :] = e
            if q == 3:
                wsum[...] += dot_t(cb[rows, :], e)
            return carry

        lax.fori_loop(0, B, embed, 0)

    def slab(ref, xc):
        return ref.at[pl.ds(pl.multiple_of(xc * 32, 32), 32)]

    def tile(ref, y):
        return ref.at[pl.ds(pl.multiple_of((y // 2) * 8, 8), 8), pl.ds(pl.multiple_of(lax.rem(y, 2) * 128, 128), 128)]

    wb[...] = wsum[...].astype(BF)
    w1[mxc] = slab(wb, mxc)[...]
    row_send(lambda xc: slab(wb, xc), w1.at[mxc], s_w1)
    sum_z()

    def forward(b, carry):
        e = eb[batch_rows(b), :]
        ef = e.astype(F32)
        pj = dot(proj_t[...], e).astype(BF)
        for i in range(4):
            bdp[i * RANK : (i + 1) * RANK, i * 256 : (i + 1) * 256] = pj
        ep = dot(q_fm, e).astype(BF)
        ecat = jnp.concatenate([ep[i * 64 : (i + 1) * 64] for i in range(4)], 1)
        x = dot_t(ecat, bdp[...])
        mean = jnp.sum(x, keepdims=True) / (NTOK * RANK)
        xc = x - mean
        var = jnp.sum(xc * xc, keepdims=True) / (NTOK * RANK)
        xn = xc * lax.rsqrt(var + 1e-05)
        for i in range(3):
            fplane[i, pl.ds(pl.multiple_of(b * 64, 64), 64), :] = xn[:, i * 128 : (i + 1) * 128]
        ra, rb = pltpu.roll(ef[:, 0:128], 64, 1), pltpu.roll(ef[:, 128:256], 64, 1)
        bdc[0:256, 0:256] = e
        bdc[256:512, 128:256] = jnp.where(low, 0.0, ra).astype(BF)
        bdc[256:512, 256:384] = jnp.where(low, ra, rb).astype(BF)
        y = dot(weo[...], bdc[...])
        for i in range(3):
            mplane[i, pl.ds(pl.multiple_of(b * 128, 128), 128), :] = y[:, i * 128 : (i + 1) * 128]
        return carry

    lax.fori_loop(0, 4, forward, 0)
    wait(w1.at[pl.ds(0, 7)], s_w1.at[1])
    wpart[...] = jnp.sum(w1[...].astype(F32), axis=0)
    w2[my] = tile(wpart, my)[...]
    column_send(lambda y: tile(wpart, y), w2.at[my], s_w2)
    lax.fori_loop(4, 5, forward, 0)
    got(1)
    hand(5).start()
    hand(6).start()
    got(2)
    hand(7).start()
    hand(8).start()
    wait(w2.at[pl.ds(0, 7)], s_w2.at[1])
    wtile[...] = jnp.sum(w2[...], axis=0)
    wzrecv[z] = wtile[...]
    z_send(lambda p: wtile, wzrecv.at[z], s_wz)
    got(0)
    hand(9).start()
    hand(10).start()
    lax.fori_loop(5, 8, forward, 0)
    wait(wzrecv.at[pl.ds(0, NZ - 1)], s_wz.at[1])
    tile(wquart, my)[...] = jnp.sum(wzrecv[...], axis=0) / SAMPLES
    column_send(lambda y: tile(wquart, my), tile(wquart, my), s_w4)

    def out_fm(q, carry):
        for i in range(3):
            at = pl.multiple_of(q * 384 + i * 128, 128)
            fm_o[:, pl.ds(at, 128)] = fplane[i, pl.ds(q, B, stride=64), :].astype(BF)
        return carry

    lax.fori_loop(0, 64, out_fm, 0, unroll=8)

    store_fm = pltpu.make_async_copy(fm_o, fm_h, s_out.at[0])
    store_fm.start()
    wait(w2.at[pl.ds(0, 7)], s_w4.at[1])
    wq[...] = wquart[...].astype(BF)
    slab(wfull, mxc)[...] = wq[...]
    row_send(lambda xc: wq, slab(wfull, mxc), s_w5)

    def out_comp(q, carry):
        for i in range(3):
            at = pl.multiple_of(q * 384 + i * 128, 128)
            comp_o[:, pl.ds(at, 128)] = mplane[i, pl.ds(q, B, stride=128), :].astype(BF)
        return carry

    lax.fori_loop(0, 128, out_comp, 0, unroll=8)

    store_comp = pltpu.make_async_copy(comp_o, comp_h, s_out.at[1])
    store_comp.start()
    for k in range(3, 11):
        got(k)
    tg_o[...] = zfull[...].astype(F32)
    store_tg = pltpu.make_async_copy(tg_o, tg_h, s_out.at[2])
    store_tg.start()
    wait(w1.at[pl.ds(0, 7)], s_w5.at[1])
    wg_o[...] = wfull[...].astype(F32)
    store_wg = pltpu.make_async_copy(wg_o, wg_h, s_out.at[3])
    store_wg.start()

    wait(reqs.at[pl.ds(0, 7)], s_rq.at[0])
    wait(reqr.at[pl.ds(0, 7)], s_rq2.at[0])
    wait(bsend.at[pl.ds(0, NP - 1)], s_b.at[0])
    wait(asend.at[pl.ds(0, NP - 1)], s_as)
    wait(zsend.at[pl.ds(0, NZ - 1)], s_z.at[0])
    wait(w1.at[pl.ds(0, 7)], s_w1.at[0])
    wait(w2.at[pl.ds(0, 7)], s_w2.at[0])
    wait(wzrecv.at[pl.ds(0, NZ - 1)], s_wz.at[0])
    wait(w2.at[pl.ds(0, 7)], s_w4.at[0])
    wait(w1.at[pl.ds(0, 7)], s_w5.at[0])
    for k in range(11):
        hand(k).wait_send()
    store_fm.wait()
    store_comp.wait()
    store_tg.wait()
    store_wg.wait()


def deliver(fm_i, comp_i, tg_i, wg_i, fm_o, comp_o, tg_o, wg_o, fm_v, comp_v, tg_v, wg_v, sems):
    held = [(comp_i, comp_v, comp_o), (tg_i, tg_v, tg_o), (fm_i, fm_v, fm_o), (wg_i, wg_v, wg_o)]
    loads = [pltpu.make_async_copy(src, mid, sems.at[0, i]) for i, (src, mid, _) in enumerate(held)]
    stores = [pltpu.make_async_copy(mid, dst, sems.at[1, i]) for i, (_, mid, dst) in enumerate(held)]
    for load in loads:
        load.start()
    for load, store in zip(loads, stores):
        load.wait()
        store.start()
    for store in stores:
        store.wait()


def on_device(emb_table, requests, token_slot, kept_mask, fm_proj, comp_weight, comp_cotangent):
    shapes = (
        jax.ShapeDtypeStruct((B, NTOK * RANK), BF),
        jax.ShapeDtypeStruct((B, NCOMP * D), BF),
        jax.ShapeDtypeStruct((D, ROWS), F32),
        jax.ShapeDtypeStruct((NCOMP, NTOK), F32),
    )
    hbm = pl.BlockSpec(memory_space=pl.ANY)
    v = pltpu.VMEM
    dma2 = pltpu.SemaphoreType.DMA((2,))
    outs = pl.pallas_call(
        kernel,
        out_shape=shapes,
        in_specs=[hbm] * 7,
        out_specs=(hbm,) * 4,
        scratch_shapes=[
            v((B, NTOK * RANK), BF), v((B, NCOMP * D), BF),
            v((D, ROWS), BF), v((CAP, NP), jnp.int32), v((1, TOK), jnp.int32), v((B, NTOK), jnp.int32),
            v((RANK, NTOK), BF), v((NCOMP, NTOK), BF), v((B, NCOMP * D), BF),
            v((8, 8, 1, 128), jnp.int32), v((8, 8, 1, 128), jnp.int32), v((8, 8, 1, 128), jnp.int32),
            v((16, 128), jnp.int32), v((16, 128, 128), jnp.int32),
            v((B, NTOK), jnp.int32), v((B, NTOK, 128), jnp.int32), v((4, TOK, 512), BF),
            v((2, TOK, 128), F32), v((TOK, 256), BF), v((TOK, 256), BF),
            v((ROWS, 256), BF), v((256, 256), BF),
            v((NP, PACK, 128), BF), v((NP, PACK, 128), BF),
            v((NP, PACK, 128), BF), v((NP, PACK, 128), BF),
            v((TOK, 256), BF), v((512, 256), BF),
            v((NZ, 16, ROWS), F32), v((NZ, 16, ROWS), BF),
            v((NZ, 16, ROWS), BF), v((D, ROWS), BF),
            v((TOK, 256), BF), v((128, 512), BF), v((384, 1024), BF), v((512, 384), BF),
            v((3, 512, 128), F32), v((3, 1024, 128), F32),
            v((256, 256), F32), v((256, 256), BF), v((8, 32, 256), BF), v((32, 256), F32), v((8, 8, 128), F32),
            v((8, 128), F32), v((NZ, 8, 128), F32), v((32, 256), F32), v((32, 256), BF), v((256, 256), BF),
            v((NCOMP, NTOK), F32), v((D, ROWS), F32),
            pltpu.SemaphoreType.DMA((7,)), dma2, dma2, dma2, pltpu.SemaphoreType.DMA, pltpu.SemaphoreType.DMA((4,)),
            dma2, dma2, dma2, dma2, dma2, dma2,
            pltpu.SemaphoreType.DMA((12,)), pltpu.SemaphoreType.DMA((12,)), pltpu.SemaphoreType.DMA((4,)),
        ],
        compiler_params=pltpu.CompilerParams(
            collective_id=0, has_side_effects=True, vmem_limit_bytes=62 * 1024 * 1024
        ),
    )(
        emb_table.T, requests[0].T, token_slot, kept_mask, fm_proj.T, comp_weight, comp_cotangent
    )
    fm, comp, tg_t, wg = pl.pallas_call(
        deliver,
        out_shape=shapes,
        in_specs=[hbm] * 4,
        out_specs=(hbm,) * 4,
        scratch_shapes=[v(x.shape, x.dtype) for x in shapes] + [pltpu.SemaphoreType.DMA((2, 4))],
        compiler_params=pltpu.CompilerParams(vmem_limit_bytes=62 * 1024 * 1024),
    )(*outs)
    return fm, comp, tg_t.T, wg


def solution(mesh):
    return jax.shard_map(
        on_device,
        mesh=mesh,
        in_specs=(
            P("emb", None),
            P(("dp", "emb"), None, None),
            P(("dp", "emb"), None),
            P(("dp", "emb"), None),
            P(),
            P(),
            P(("dp", "emb"), None),
        ),
        out_specs=(P(("dp", "emb"), None), P(("dp", "emb"), None), P("emb", None), P()),
        check_vma=False,
    )
```

```python
import functools

import jax
import jax.numpy as jnp
from jax import lax
from jax.experimental import pallas as pl
from jax.experimental.pallas import tpu as pltpu
from jax.sharding import PartitionSpec as P

MESH = pl.DeviceIdType.MESH
BF = jnp.bfloat16
F32 = jnp.float32
NZ, NY, NX, NC = 12, 8, 4, 2
NP = NY * NX * NC
D, NTOK, RANK, NCOMP, B, ROWS, CAP = 192, 256, 96, 256, 8, 1024, 32
TOK = B * NTOK
PACK = CAP + CAP // 2
SAMPLES = 6144


def dot(a, b):
    return jnp.dot(a, b, preferred_element_type=F32)


def dot_t(a, b):
    return lax.dot_general(a, b, (((1,), (1,)), ((), ())), preferred_element_type=F32)


def onehot(mask):
    return mask.astype(F32).astype(BF)


def alternate(e, n):
    half = (e + 1) // 2
    return lax.rem(jnp.where(lax.rem(e, 2) == 1, half, n - half), n)


def far_first(e):
    return alternate(15 - e, 16)


def kernel(
    table_h, req_h, slot_h, mask_h, proj_h, weight_h, cot_h,
    fm_h, comp_h, tg_h, wg_h,
    fm_o, comp_o,
    table_t, req_t, slot, mask, proj_t, weight, cot,
    reqs, reqm, reqr, wrow, wcol, slot8, keyb, pq,
    cplane, cb, rg, table, wt,
    bsend, brecv, asend, arecv, ret, arr,
    tgf, zsend, zrecv, zfull,
    eb, weo, bdp, bdc, fplane, mplane,
    wsum, wb, w1, wpart, w2, wtile, wzrecv, wquart, wq, wfull, wg_o, tg_o,
    s_in, s_rq, s_rq2, s_b, s_as, s_ar, s_z, s_w1, s_w2, s_wz, s_w4, s_w5, s_gs, s_gr, s_out,
):
    loads = [
        pltpu.make_async_copy(src, dst, s_in.at[i])
        for i, (src, dst) in enumerate([
            (req_h, req_t), (slot_h, slot), (mask_h, mask), (cot_h, cot),
            (weight_h, weight), (table_h, table_t), (proj_h, proj_t),
        ])
    ]
    for load in loads:
        load.start()
    z = lax.axis_index("dp")
    me = lax.axis_index("emb")
    my = me // (NX * NC)
    mx = lax.rem(me // NC, NX)
    mc = lax.rem(me, NC)

    def peer(j):
        dy = alternate(lax.rem(j, NY), NY)
        dxc = j // NY
        py = lax.rem(my + dy, NY)
        px = lax.rem(mx + dxc // NC, NX)
        pc = lax.rem(mc + dxc, NC)
        return (py * NX + px) * NC + pc

    def zpeer(j):
        return lax.rem(z + alternate(j, NZ), NZ)

    def wait(ref, sem):
        pltpu.make_async_copy(ref, ref, sem).wait()

    mxc = lax.rem(me, NX * NC)

    def row_peer(k):
        return lax.rem(mxc + k, NX * NC)

    def row_send(src, dst, sems):
        for k in range(1, NX * NC):
            xc = row_peer(k)
            pltpu.make_async_remote_copy(
                src_ref=src(xc), dst_ref=dst, send_sem=sems.at[0], recv_sem=sems.at[1],
                device_id={"emb": my * NX * NC + xc}, device_id_type=MESH,
            ).start()

    def column_send(src, dst, sems):
        for k in range(1, NY):
            y = lax.rem(my + alternate(jnp.int32(k), NY), NY)
            pltpu.make_async_remote_copy(
                src_ref=src(y), dst_ref=dst, send_sem=sems.at[0], recv_sem=sems.at[1],
                device_id={"emb": y * NX * NC + mxc}, device_id_type=MESH,
            ).start()

    def z_send(src, dst, sems):
        def body(j, carry):
            p = zpeer(j)
            pltpu.make_async_remote_copy(
                src_ref=src(p), dst_ref=dst, send_sem=sems.at[0], recv_sem=sems.at[1],
                device_id={"dp": p}, device_id_type=MESH,
            ).start()
            return carry
        lax.fori_loop(1, NZ, body, 0)

    barrier = pltpu.get_barrier_semaphore()

    def sig_plane(j, carry):
        pl.semaphore_signal(barrier, inc=1, device_id={"emb": peer(j)}, device_id_type=MESH)
        return carry

    def sig_z(j, carry):
        pl.semaphore_signal(barrier, inc=1, device_id={"dp": zpeer(j)}, device_id_type=MESH)
        return carry

    lax.fori_loop(1, NP, sig_plane, 0, unroll=3)
    lax.fori_loop(1, NZ, sig_z, 0)

    lane = lax.broadcasted_iota(jnp.int32, (1, 128), 1)
    low = lane < 64

    for load in loads[:3]:
        load.wait()

    rt = jnp.concatenate([req_t[...], jnp.zeros((128 - CAP, NP), jnp.int32)], 0)
    rt = jnp.concatenate([rt, jnp.zeros((128, 128 - NP), jnp.int32)], 1).T
    rt = rt[0:NP]
    tiled = rt
    for i in range(1, 4):
        tiled = tiled + pltpu.roll(rt, 32 * i, 1)
    tiled = jnp.where(lane // CAP == lax.rem(me, 4), tiled, 0)
    for p in range(NP):
        reqs[p % 8, p // 8] = tiled[p : p + 1]

    for b in range(B):
        slot8[b : b + 1, :] = slot[0:1, b * NTOK : (b + 1) * NTOK]
    masked = jnp.where(mask[...] > 0, slot8[...], -1)
    slot8[...] = masked

    loads[3].wait()
    loads[4].wait()

    def unpack_cot(mp, carry):
        at = pl.multiple_of(mp * 384, 128)
        x = cot[:, pl.ds(at, 384)].astype(F32)
        x0, x1, x2 = x[:, 0:128], x[:, 128:256], x[:, 256:384]
        r1 = pltpu.roll(x1, 64, 1)
        r2 = pltpu.roll(x2, 64, 1)
        ev, od = pl.ds(2 * mp, B, stride=NCOMP), pl.ds(2 * mp + 1, B, stride=NCOMP)
        cplane[0, ev, :] = x0
        cplane[1, ev, :] = jnp.where(low, x1, r1)
        cplane[0, od, :] = jnp.where(low, r1, r2)
        cplane[1, od, :] = jnp.where(low, r2, x2)
        return carry

    lax.fori_loop(0, NCOMP // 2, unpack_cot, 0, unroll=8)
    wt[...] = weight[...].astype(F32).T.astype(BF)

    def make_rg(b, carry):
        rows = pl.ds(pl.multiple_of(b * NCOMP, NCOMP), NCOMP)
        c = jnp.concatenate([cplane[0, rows, :], cplane[1, rows, :]], 1).astype(BF)
        cb[rows, :] = c
        rg[rows, :] = dot(wt[...], c).astype(BF)
        return carry

    lax.fori_loop(0, B, make_rg, 0)

    pl.semaphore_wait(barrier, NP - 1 + NZ - 1)
    reqm[:, mxc] = reqs[mxc]
    row_send(lambda xc: reqs.at[xc], reqm.at[:, mxc], s_rq)

    sub = lax.broadcasted_iota(jnp.int32, (128, 1), 0)

    def send4(buf, dst, g, send_sem, recv_sem):
        for q in range(4):
            p = g * 4 + lax.rem(me + q, 4)

            @pl.when(p != me)
            def _():
                pltpu.make_async_remote_copy(
                    src_ref=buf.at[p], dst_ref=dst, send_sem=send_sem, recv_sem=recv_sem,
                    device_id={"emb": p}, device_id_type=MESH,
                ).start()

    def packed(val, dst, g):
        for q in range(4):
            v = val[q * CAP : (q + 1) * CAP]
            dst[g * 4 + q, 0:CAP, :] = v[:, 0:128].astype(BF)
            dst[g * 4 + q, CAP:PACK, :] = jnp.where(low, v[0:16, 128:256], v[16:32, 128:256]).astype(BF)

    def order(e, carry):
        g = lax.rem(me // 4 + far_first(e), 16)
        key = sub + g * 128
        pt = jnp.concatenate([onehot(slot8[b : b + 1, :] == key) for b in range(B)], 1)
        packed(dot(pt, rg[...]), bsend, g)
        send4(bsend, brecv.at[me], g, s_b.at[0], s_b.at[1])
        return carry

    lax.fori_loop(0, 6, order, 0)
    wait(reqs.at[pl.ds(0, 7)], s_rq.at[1])
    reqr[my] = reqm[my]
    column_send(lambda y: reqm.at[y], reqr.at[my], s_rq2)
    lax.fori_loop(6, 16, order, 0)
    brecv[me] = bsend[me]

    loads[5].wait()
    for i in range(8):
        blk = table_t[:, i * 128 : (i + 1) * 128].astype(F32)
        blk = jnp.concatenate([blk, blk[128:192]], 0).T
        table[i * 128 : (i + 1) * 128, :] = blk.astype(BF)

    wait(reqr.at[pl.ds(0, 7)], s_rq2.at[1])
    for g in range(16):
        y, h = g // 2, (g % 2) * 4
        wrow[g : g + 1, :] = reqr[y, h] + reqr[y, h + 1] + reqr[y, h + 2] + reqr[y, h + 3]
    wc = jnp.concatenate([wrow[...], jnp.zeros((112, 128), jnp.int32)], 0).T
    for g in range(16):
        wcol[g] = jnp.broadcast_to(wc[:, g : g + 1], (128, 128))
    rlane = lax.broadcasted_iota(jnp.int32, (1, 128), 1)

    def fetch(e, carry):
        g = lax.rem(me // 4 + far_first(e), 16)
        col = wcol[g]
        o = jnp.concatenate([onehot(col == rlane + 128 * i) for i in range(8)], 1)
        packed(dot(o, table[...]), asend, g)
        send4(asend, arecv.at[me], g, s_as, s_ar.at[e // 4])
        return carry

    lax.fori_loop(0, 16, fetch, 0)
    arecv[me] = asend[me]

    def group_from(e):
        return lax.rem(me // 4 - far_first(e) + 16, 16)

    km = jnp.concatenate([slot8[...], jnp.full((120, NTOK), -1, jnp.int32)], 0).T
    for b in range(B):
        keyb[b] = jnp.broadcast_to(km[:, b : b + 1], (NTOK, 128))

    def choose(k, carry):
        q, b = k // B, lax.rem(k, B)
        key = keyb[b]
        o = [onehot(key == rlane + 128 * group_from(4 * q + i)) for i in range(4)]
        pq[q, pl.ds(pl.multiple_of(b * NTOK, NTOK), NTOK), :] = jnp.concatenate(o, 1)
        return carry

    lax.fori_loop(0, 4 * B, choose, 0)

    def unpack_one(src, p, dst, at):
        dst[pl.ds(at, CAP), 0:128] = src[p, 0:CAP, :]
        h = src[p, CAP:PACK, :].astype(F32)
        dst[pl.ds(at, 16), 128:256] = jnp.where(low, h, 0.0).astype(BF)
        h = pltpu.roll(h, 64, 1)
        dst[pl.ds(pl.multiple_of(at + 16, 16), 16), 128:256] = jnp.where(low, h, 0.0).astype(BF)

    wait(brecv.at[pl.ds(0, NP - 1)], s_b.at[1])

    def unpack_ret(p, carry):
        unpack_one(brecv, p, ret, pl.multiple_of(p * CAP, CAP))
        return carry

    lax.fori_loop(0, NP, unpack_ret, 0, unroll=4)

    sub2 = lax.broadcasted_iota(jnp.int32, (256, 1), 0)

    def scatter(rb, carry):
        key = sub2 + rb * 256
        o = jnp.concatenate([onehot(wrow[g : g + 1, :] == key) for g in range(16)], 1)
        t = dot(o, ret[...])
        t = t.T[0:D].reshape(NZ, 16, 256)
        at = pl.ds(pl.multiple_of(rb * 256, 256), 256)
        tgf[:, :, at] = t
        zsend[:, :, at] = t.astype(BF)
        return carry

    for h in range(2):
        lax.fori_loop(2 * h, 2 * h + 2, scatter, 0)
        half = pl.ds(512 * h, 512)
        z_send(lambda p: zsend.at[p, :, half], zrecv.at[z, :, half], s_z)

    def zpart(c):
        return zfull.at[pl.ds(pl.multiple_of(lax.rem(c + NZ, NZ) * 16, 16), 16)]

    steps = [
        (0, 6), (0, 3), (0, -3), (0, 1), (0, -1),
        (-3, 1), (-3, -1), (3, 1), (3, -1), (6, 1), (6, -1),
    ]

    def hand(k):
        a, d = steps[k]
        return pltpu.make_async_remote_copy(
            src_ref=zpart(z + a), dst_ref=zpart(z + a), send_sem=s_gs.at[k], recv_sem=s_gr.at[k],
            device_id={"dp": lax.rem(z + d + NZ, NZ)}, device_id_type=MESH,
        )

    def got(k):
        a, d = steps[k]
        wait(zpart(z - d + a), s_gr.at[k])

    def sum_z():
        wait(zrecv.at[pl.ds(0, NZ - 1)], s_z.at[1])
        zrecv[z] = jnp.zeros((16, ROWS), BF)
        acc = tgf[z]
        for i in range(NZ):
            acc = acc + zrecv[i].astype(F32)
        zpart(z)[...] = acc.astype(BF)
        for k in range(5):
            hand(k).start()

    r256 = lax.broadcasted_iota(jnp.int32, (256, 256), 0)
    c256 = lax.broadcasted_iota(jnp.int32, (256, 256), 1)
    q_fm = onehot(c256 == 4 * lax.rem(r256, 64) + r256 // 64)
    q_w = onehot(c256 == 2 * lax.rem(r256, 128) + r256 // 128)
    wp = dot(q_w, weight[...]).astype(BF)
    weo[...] = jnp.concatenate([wp[0:128], wp[128:256]], 1)
    bdp[...] = jnp.zeros_like(bdp)
    bdc[...] = jnp.zeros_like(bdc)
    loads[6].wait()
    wsum[...] = jnp.zeros_like(wsum)

    def batch_rows(b):
        return pl.ds(pl.multiple_of(b * NTOK, NTOK), NTOK)

    for q in range(4):
        wait(arecv.at[pl.ds(0, 15 if q == 3 else 16)], s_ar.at[q])

        def unpack_arr(k, carry):
            i, c = k // 4, lax.rem(k, 4)
            unpack_one(arecv, group_from(4 * q + i) * 4 + c, arr, pl.multiple_of(k * CAP, CAP))
            return carry

        lax.fori_loop(0, 16, unpack_arr, 0, unroll=4)

        def embed(b, carry):
            rows = batch_rows(b)
            e = dot(pq[q, rows, :], arr[...])
            if q > 0:
                e = e + eb[rows, :].astype(F32)
            e = e.astype(BF)
            eb[rows, :] = e
            if q == 3:
                wsum[...] += dot_t(cb[rows, :], e)
            return carry

        lax.fori_loop(0, B, embed, 0)

    def slab(ref, xc):
        return ref.at[pl.ds(pl.multiple_of(xc * 32, 32), 32)]

    def tile(ref, y):
        return ref.at[pl.ds(pl.multiple_of((y // 2) * 8, 8), 8), pl.ds(pl.multiple_of(lax.rem(y, 2) * 128, 128), 128)]

    wb[...] = wsum[...].astype(BF)
    w1[mxc] = slab(wb, mxc)[...]
    row_send(lambda xc: slab(wb, xc), w1.at[mxc], s_w1)
    sum_z()

    def forward(b, carry):
        e = eb[batch_rows(b), :]
        ef = e.astype(F32)
        pj = dot(proj_t[...], e).astype(BF)
        for i in range(4):
            bdp[i * RANK : (i + 1) * RANK, i * 256 : (i + 1) * 256] = pj
        ep = dot(q_fm, e).astype(BF)
        ecat = jnp.concatenate([ep[i * 64 : (i + 1) * 64] for i in range(4)], 1)
        x = dot_t(ecat, bdp[...])
        mean = jnp.sum(x, keepdims=True) / (NTOK * RANK)
        xc = x - mean
        var = jnp.sum(xc * xc, keepdims=True) / (NTOK * RANK)
        xn = xc * lax.rsqrt(var + 1e-05)
        for i in range(3):
            fplane[i, pl.ds(pl.multiple_of(b * 64, 64), 64), :] = xn[:, i * 128 : (i + 1) * 128]
        ra, rb = pltpu.roll(ef[:, 0:128], 64, 1), pltpu.roll(ef[:, 128:256], 64, 1)
        bdc[0:256, 0:256] = e
        bdc[256:512, 128:256] = jnp.where(low, 0.0, ra).astype(BF)
        bdc[256:512, 256:384] = jnp.where(low, ra, rb).astype(BF)
        y = dot(weo[...], bdc[...])
        for i in range(3):
            mplane[i, pl.ds(pl.multiple_of(b * 128, 128), 128), :] = y[:, i * 128 : (i + 1) * 128]
        return carry

    lax.fori_loop(0, 3, forward, 0)
    wait(w1.at[pl.ds(0, 7)], s_w1.at[1])
    wpart[...] = jnp.sum(w1[...].astype(F32), axis=0)
    w2[my] = tile(wpart, my)[...]
    column_send(lambda y: tile(wpart, y), w2.at[my], s_w2)
    lax.fori_loop(3, 5, forward, 0)
    wait(w2.at[pl.ds(0, 7)], s_w2.at[1])
    wtile[...] = jnp.sum(w2[...], axis=0)
    wzrecv[z] = wtile[...]
    z_send(lambda p: wtile, wzrecv.at[z], s_wz)
    got(1)
    hand(5).start()
    hand(6).start()
    got(2)
    hand(7).start()
    hand(8).start()
    got(0)
    hand(9).start()
    hand(10).start()
    lax.fori_loop(5, 8, forward, 0)
    wait(wzrecv.at[pl.ds(0, NZ - 1)], s_wz.at[1])
    tile(wquart, my)[...] = jnp.sum(wzrecv[...], axis=0) / SAMPLES
    column_send(lambda y: tile(wquart, my), tile(wquart, my), s_w4)

    def out_fm(q, carry):
        for i in range(3):
            at = pl.multiple_of(q * 384 + i * 128, 128)
            fm_o[:, pl.ds(at, 128)] = fplane[i, pl.ds(q, B, stride=64), :].astype(BF)
        return carry

    lax.fori_loop(0, 64, out_fm, 0, unroll=8)

    store_fm = pltpu.make_async_copy(fm_o, fm_h, s_out.at[0])
    store_fm.start()
    wait(w2.at[pl.ds(0, 7)], s_w4.at[1])
    wq[...] = wquart[...].astype(BF)
    slab(wfull, mxc)[...] = wq[...]
    row_send(lambda xc: wq, slab(wfull, mxc), s_w5)

    def out_comp(q, carry):
        for i in range(3):
            at = pl.multiple_of(q * 384 + i * 128, 128)
            comp_o[:, pl.ds(at, 128)] = mplane[i, pl.ds(q, B, stride=128), :].astype(BF)
        return carry

    lax.fori_loop(0, 128, out_comp, 0, unroll=8)

    store_comp = pltpu.make_async_copy(comp_o, comp_h, s_out.at[1])
    store_comp.start()
    for k in range(3, 11):
        got(k)
    tg_o[...] = zfull[...].astype(F32)
    store_tg = pltpu.make_async_copy(tg_o, tg_h, s_out.at[2])
    store_tg.start()
    wait(w1.at[pl.ds(0, 7)], s_w5.at[1])
    wg_o[...] = wfull[...].astype(F32)
    store_wg = pltpu.make_async_copy(wg_o, wg_h, s_out.at[3])
    store_wg.start()

    wait(reqs.at[pl.ds(0, 7)], s_rq.at[0])
    wait(reqr.at[pl.ds(0, 7)], s_rq2.at[0])
    wait(bsend.at[pl.ds(0, NP - 1)], s_b.at[0])
    wait(asend.at[pl.ds(0, NP - 1)], s_as)
    wait(zsend.at[pl.ds(0, NZ - 1)], s_z.at[0])
    wait(w1.at[pl.ds(0, 7)], s_w1.at[0])
    wait(w2.at[pl.ds(0, 7)], s_w2.at[0])
    wait(wzrecv.at[pl.ds(0, NZ - 1)], s_wz.at[0])
    wait(w2.at[pl.ds(0, 7)], s_w4.at[0])
    wait(w1.at[pl.ds(0, 7)], s_w5.at[0])
    for k in range(11):
        hand(k).wait_send()
    store_fm.wait()
    store_comp.wait()
    store_tg.wait()
    store_wg.wait()


def deliver(fm_i, comp_i, tg_i, wg_i, fm_o, comp_o, tg_o, wg_o, fm_v, comp_v, tg_v, wg_v, sems):
    held = [(comp_i, comp_v, comp_o), (tg_i, tg_v, tg_o), (fm_i, fm_v, fm_o), (wg_i, wg_v, wg_o)]
    loads = [pltpu.make_async_copy(src, mid, sems.at[0, i]) for i, (src, mid, _) in enumerate(held)]
    stores = [pltpu.make_async_copy(mid, dst, sems.at[1, i]) for i, (_, mid, dst) in enumerate(held)]
    for load in loads:
        load.start()
    for load, store in zip(loads, stores):
        load.wait()
        store.start()
    for store in stores:
        store.wait()


def on_device(emb_table, requests, token_slot, kept_mask, fm_proj, comp_weight, comp_cotangent):
    shapes = (
        jax.ShapeDtypeStruct((B, NTOK * RANK), BF),
        jax.ShapeDtypeStruct((B, NCOMP * D), BF),
        jax.ShapeDtypeStruct((D, ROWS), F32),
        jax.ShapeDtypeStruct((NCOMP, NTOK), F32),
    )
    hbm = pl.BlockSpec(memory_space=pl.ANY)
    v = pltpu.VMEM
    dma2 = pltpu.SemaphoreType.DMA((2,))
    outs = pl.pallas_call(
        kernel,
        out_shape=shapes,
        in_specs=[hbm] * 7,
        out_specs=(hbm,) * 4,
        scratch_shapes=[
            v((B, NTOK * RANK), BF), v((B, NCOMP * D), BF),
            v((D, ROWS), BF), v((CAP, NP), jnp.int32), v((1, TOK), jnp.int32), v((B, NTOK), jnp.int32),
            v((RANK, NTOK), BF), v((NCOMP, NTOK), BF), v((B, NCOMP * D), BF),
            v((8, 8, 1, 128), jnp.int32), v((8, 8, 1, 128), jnp.int32), v((8, 8, 1, 128), jnp.int32),
            v((16, 128), jnp.int32), v((16, 128, 128), jnp.int32),
            v((B, NTOK), jnp.int32), v((B, NTOK, 128), jnp.int32), v((4, TOK, 512), BF),
            v((2, TOK, 128), F32), v((TOK, 256), BF), v((TOK, 256), BF),
            v((ROWS, 256), BF), v((256, 256), BF),
            v((NP, PACK, 128), BF), v((NP, PACK, 128), BF),
            v((NP, PACK, 128), BF), v((NP, PACK, 128), BF),
            v((TOK, 256), BF), v((512, 256), BF),
            v((NZ, 16, ROWS), F32), v((NZ, 16, ROWS), BF),
            v((NZ, 16, ROWS), BF), v((D, ROWS), BF),
            v((TOK, 256), BF), v((128, 512), BF), v((384, 1024), BF), v((512, 384), BF),
            v((3, 512, 128), F32), v((3, 1024, 128), F32),
            v((256, 256), F32), v((256, 256), BF), v((8, 32, 256), BF), v((32, 256), F32), v((8, 8, 128), F32),
            v((8, 128), F32), v((NZ, 8, 128), F32), v((32, 256), F32), v((32, 256), BF), v((256, 256), BF),
            v((NCOMP, NTOK), F32), v((D, ROWS), F32),
            pltpu.SemaphoreType.DMA((7,)), dma2, dma2, dma2, pltpu.SemaphoreType.DMA, pltpu.SemaphoreType.DMA((4,)),
            dma2, dma2, dma2, dma2, dma2, dma2,
            pltpu.SemaphoreType.DMA((12,)), pltpu.SemaphoreType.DMA((12,)), pltpu.SemaphoreType.DMA((4,)),
        ],
        compiler_params=pltpu.CompilerParams(
            collective_id=0, has_side_effects=True, vmem_limit_bytes=62 * 1024 * 1024
        ),
    )(
        emb_table.T, requests[0].T, token_slot, kept_mask, fm_proj.T, comp_weight, comp_cotangent
    )
    fm, comp, tg_t, wg = pl.pallas_call(
        deliver,
        out_shape=shapes,
        in_specs=[hbm] * 4,
        out_specs=(hbm,) * 4,
        scratch_shapes=[v(x.shape, x.dtype) for x in shapes] + [pltpu.SemaphoreType.DMA((2, 4))],
        compiler_params=pltpu.CompilerParams(vmem_limit_bytes=62 * 1024 * 1024),
    )(*outs)
    return fm, comp, tg_t.T, wg


def solution(mesh):
    return jax.shard_map(
        on_device,
        mesh=mesh,
        in_specs=(
            P("emb", None),
            P(("dp", "emb"), None, None),
            P(("dp", "emb"), None),
            P(("dp", "emb"), None),
            P(),
            P(),
            P(("dp", "emb"), None),
        ),
        out_specs=(P(("dp", "emb"), None), P(("dp", "emb"), None), P("emb", None), P()),
        check_vma=False,
    )
```
